32 devices in a mesh: outer: 2 (over core), nodes: 16 (over z, y, x).
Axes of the slice: x: 2, y: 2, z: 4, core: 2. Of those that a mesh axis runs over, the one named last changes fastest.
Arguments:
- features: bfloat16 [16384, 512], P(('outer', 'nodes')), may hold values from -6 to 6
- w_query: bfloat16 [512, 512], replicated, may hold values from -0.25 to 0.25
- w_key: bfloat16 [512, 512], replicated, may hold values from -0.75 to 0.75
- w_value: bfloat16 [512, 512], replicated, may hold values from -0.25 to 0.25
- bases: bfloat16 [2, 512, 512], replicated, may hold values from -0.09375 to 0.09375
- rel_coef: float32 [8, 2], replicated, may hold values from -4 to 4
- send_rows: int32 [32, 16, 32], P(('outer', 'nodes')), may hold values from 0 to 511
- tile_src: int32 [32, 8, 4, 128], P(('outer', 'nodes')), may hold values from 0 to 1023, as said below
- tile_dst: int32 [32, 8, 4, 128], P(('outer', 'nodes')), may hold values from 0 to 127
- tile_count: int32 [32, 8, 4], P(('outer', 'nodes')), may hold values from 1 to 128, as said below
- cotangent: float32 [16384, 512], P(('outer', 'nodes')), may hold values from -6 to 6
Outputs:
- layer_out: float32 [16384, 512], P(('outer', 'nodes'))
- grad_x: float32 [16384, 512], P(('outer', 'nodes'))
- query_grad: float32 [512, 512], replicated
- key_grad: float32 [512, 512], replicated
- value_grad: float32 [512, 512], replicated
- bases_grad: float32 [2, 512, 512], replicated
- coef_grad: float32 [8, 2], replicated
The draws below stay inside these ranges and needn't reach their ends.
Inputs may be any that keep to these rules, and one draw needn't show every extreme that they name: `send_rows`: row indices into the sending device's own 512 rows. `tile_src`: rows of the device's table (its own 512 rows, then 32 slots from each node position of its group in order). Edges read only slots of other devices of the group, and of each sender only its first slots, as many as that sender fills for this device, between 1 and 32. The first tile_count slots of a tile hold its edges. Every device has a tile with all 128 slots used.
All inputs are finite; a program needn't handle non-finite values.
Results may differ from the reference program's by a relative error of at most 0.0041.
Values may be sent and summed in bfloat16 or wider, within the bound.
No kernel may reach another device: no remote copies, remote signals or barrier semaphores. Data moves between devices by JAX's collectives and lax.ppermute only.
A program may use at most 128 MiB of HBM per device.

```python
import jax
import jax.numpy as jnp
from jax import lax

D = 512
HEADS = 8
HEAD_DIM = 64
REL = 8
BASES = 2
TILE = 128
EDGE_CAP = 128
SEND_CAP = 32
NODE_DEV = 512
NODES = 16384
TILES = 4
N_NODES = 16
DEVICES = 32


def draw_tile_src(key, part):
    array_shape = (DEVICES, REL, TILES, EDGE_CAP)
    filled = jax.random.randint(jax.random.fold_in(key, 5), (DEVICES, N_NODES), 1, SEND_CAP + 1)
    sender_pos = (jnp.arange(DEVICES, dtype=jnp.int32) % N_NODES)[:, None]
    receiver_pos = jnp.arange(N_NODES, dtype=jnp.int32)[None, :]
    forced_full = (sender_pos == N_NODES - 1) & (receiver_pos == 0)
    filled = jnp.where(forced_full, SEND_CAP, filled)
    device = jnp.arange(DEVICES, dtype=jnp.int32).reshape(DEVICES, 1, 1, 1)
    group_index = device // N_NODES
    position = device % N_NODES
    subkeys = jax.random.split(jax.random.fold_in(key, 11), 4)
    local_row = jax.random.randint(subkeys[0], array_shape, 0, NODE_DEV)
    hop_count = jax.random.randint(subkeys[1], array_shape, 0, N_NODES - 1)
    peer_node = (position + 1 + hop_count) % N_NODES
    sender = group_index * N_NODES + peer_node
    filled_here = filled[sender, position]
    slot_index = jax.random.randint(subkeys[2], array_shape, 0, 1 << 20) % filled_here
    halo_row = NODE_DEV + peer_node * SEND_CAP + slot_index
    remote = jax.random.randint(subkeys[3], array_shape, 0, 2) == 1
    result = jnp.where(remote, halo_row, local_row).astype(jnp.int32)
    result = result.at[0, 0, 0, 0].set(NODE_DEV + N_NODES * SEND_CAP - 1)
    result = result.at[0, 0, 0, 1].set(0)
    return result.astype(jnp.int32)


def draw_tile_count(key, part):
    subkeys = jax.random.split(jax.random.fold_in(key, 23), 3)
    weight_level = jax.random.randint(subkeys[0], (DEVICES, REL, 1), 1, 5)
    ceiling = EDGE_CAP * weight_level // 4
    drawn = jax.random.randint(subkeys[1], (DEVICES, REL, TILES), 0, 1 << 20) % (ceiling // 2 + 1)
    counts = ceiling - drawn
    chosen = jax.random.randint(subkeys[2], (DEVICES, 1), 0, REL * TILES)
    full_tile = (jnp.arange(REL * TILES, dtype=jnp.int32)[None, :] == chosen).reshape(DEVICES, REL, TILES)
    return jnp.where(full_tile, EDGE_CAP, counts).astype(jnp.int32)


def set_ends(entries, rng, low, top_value):
    longest = entries.shape.index(max(entries.shape))
    spots = []
    for shift in (0, 1):
        where = [jax.random.randint(jax.random.fold_in(rng, axis), (), 0, length) for axis, length in enumerate(entries.shape)]
        where[longest] = (where[longest] + shift) % entries.shape[longest]
        spots.append(tuple(where))
    return entries.at[spots[0]].set(low).at[spots[1]].set(top_value)


def steps_of(rng, extent, cuts, least, high):
    loudness, own = 1.0, jax.random.fold_in(rng, 6)
    for axis_at, parts in cuts:
        heights = jnp.exp(jax.random.uniform(jax.random.fold_in(own, axis_at), (parts,), jnp.float32, least / len(cuts), high / len(cuts)))
        loudness = loudness * jnp.repeat(heights, extent[axis_at] // parts).reshape([-1 if axis == axis_at else 1 for axis in range(len(extent))])
    return loudness


def scatter_about(key, extent, deviation, most, cuts=(), held_as=jnp.bfloat16):
    values = jax.random.normal(key, extent, jnp.float32) * deviation
    if len(cuts) > 0:
        values = steps_of(key, extent, cuts, -0.22, 0.18) * values
    return jnp.clip(values, min=-most, max=most).astype(held_as)


def setup_inputs(seed: int = 0) -> dict:
    keys = jax.random.split(jax.random.key(seed), 12)
    features = scatter_about(keys[0], (NODES, D), 1.0, 6.0, ((0, 32),))
    w_query = scatter_about(keys[1], (D, D), D ** -0.5, 0.25)
    w_key = scatter_about(keys[2], (D, D), (D // 8) ** -0.5, 0.75)
    w_value = scatter_about(keys[3], (D, D), D ** -0.5, 0.25)
    bases = scatter_about(keys[4], (BASES, D, D), (REL * D) ** -0.5, 0.09375)
    rel_coef = scatter_about(keys[5], (REL, BASES), 1.0, 4.0, (), jnp.float32)
    send_rows = set_ends(jax.random.randint(keys[6], (DEVICES, N_NODES, SEND_CAP), 0, NODE_DEV), jax.random.fold_in(keys[6], 1), 0, NODE_DEV - 1).astype(jnp.int32)
    tile_src = draw_tile_src(jax.random.fold_in(keys[11], 71), 0)
    tile_dst = set_ends(jax.random.randint(keys[8], (DEVICES, REL, TILES, EDGE_CAP), 0, TILE), jax.random.fold_in(keys[8], 1), 0, TILE - 1).astype(jnp.int32)
    tile_count = draw_tile_count(jax.random.fold_in(keys[11], 71), 0)
    cotangent = scatter_about(keys[10], (NODES, D), 1.0, 6.0, ((0, 32),), jnp.float32)
    return dict(features=features, w_query=w_query, w_key=w_key, w_value=w_value, bases=bases, rel_coef=rel_coef, send_rows=send_rows, tile_src=tile_src, tile_dst=tile_dst, tile_count=tile_count, cotangent=cotangent)


precise = lax.Precision.HIGHEST


def reference(features, w_query, w_key, w_value, bases, rel_coef, send_rows, tile_src, tile_dst, tile_count, cotangent):
    table_rows = NODE_DEV + N_NODES * SEND_CAP
    norm_scale = 1.0 / (NODES ** 0.5)
    w_all = jnp.concatenate([w_query, w_key, w_value], axis=1)
    projected = jnp.dot(features, w_all, preferred_element_type=jnp.float32)
    exp_query = jnp.exp(projected[:, :D]).reshape(NODES, HEADS, HEAD_DIM)
    exp_key = jnp.exp(projected[:, D:2 * D]).reshape(NODES, HEADS, HEAD_DIM)
    values = projected[:, 2 * D:].reshape(NODES, HEADS, HEAD_DIM)
    kv_sum = jnp.einsum('ihd,ihe->hde', exp_key, values, precision=precise)
    ks_sum = jnp.sum(exp_key, axis=0)
    normalizer = jnp.einsum('ihd,hd->ih', exp_query, ks_sum, precision=precise)
    attended = jnp.einsum('ihd,hde->ihe', exp_query, kv_sum, precision=precise) / normalizer[:, :, None]
    cot_half = cotangent.astype(jnp.bfloat16)
    bases_wide = bases.astype(jnp.float32)

    def device_step(carry, device):
        graph_grad, bases_acc, coef_acc = carry
        group_index = device // N_NODES
        position = device % N_NODES
        own_rows = lax.dynamic_slice_in_dim(features, device * NODE_DEV, NODE_DEV, 0)
        senders = group_index * N_NODES + jnp.arange(N_NODES, dtype=jnp.int32)
        picks = send_rows[senders, position, :]
        global_rows = (senders[:, None] * NODE_DEV + picks).reshape(-1).astype(jnp.int32)
        halo_table = jnp.concatenate([own_rows, features[global_rows]], axis=0)
        sources = tile_src[device].reshape(-1)
        targets = tile_dst[device]
        counts = tile_count[device]
        live_mask = jnp.arange(EDGE_CAP, dtype=jnp.int32)[None, None, :] < counts[:, :, None]
        segment = (jnp.arange(REL, dtype=jnp.int32)[:, None, None] * NODE_DEV
                   + jnp.arange(TILES, dtype=jnp.int32)[None, :, None] * TILE + targets).reshape(-1).astype(jnp.int32)
        live_wide = live_mask.reshape(-1).astype(jnp.float32)
        gathered = halo_table[sources].astype(jnp.float32) * live_wide[:, None]
        row_sums = jax.ops.segment_sum(gathered, segment, num_segments=REL * NODE_DEV).reshape(REL, NODE_DEV, D)
        degree = jnp.maximum(jax.ops.segment_sum(live_wide, segment, num_segments=REL * NODE_DEV), 1.0).reshape(REL, NODE_DEV)
        aggregate = row_sums / degree[:, :, None]
        basis_in = jnp.einsum('rb,rmd->bmd', rel_coef, aggregate, precision=precise).astype(jnp.bfloat16)
        basis_wide = basis_in.astype(jnp.float32)
        conv_out = jnp.einsum('bmd,bde->me', basis_wide, bases_wide, precision=precise)
        cot_dev = lax.dynamic_slice_in_dim(cot_half, device * NODE_DEV, NODE_DEV, 0).astype(jnp.float32)
        basis_grad = jnp.einsum('me,bde->bmd', cot_dev, bases_wide, precision=precise)
        bases_acc = bases_acc + jnp.einsum('bmd,me->bde', basis_wide, cot_dev, precision=precise)
        coef_acc = coef_acc + jnp.einsum('rmd,bmd->rb', aggregate, basis_grad, precision=precise)
        agg_grad = jnp.einsum('rb,bmd->rmd', rel_coef, basis_grad, precision=precise) / degree[:, :, None]
        moved = agg_grad.reshape(-1, D)[segment] * live_wide[:, None]
        table_grad = jax.ops.segment_sum(moved, sources, num_segments=table_rows)
        own_grad = lax.dynamic_slice_in_dim(graph_grad, device * NODE_DEV, NODE_DEV, 0) + table_grad[:NODE_DEV]
        graph_grad = lax.dynamic_update_slice_in_dim(graph_grad, own_grad, device * NODE_DEV, 0)
        graph_grad = graph_grad.at[global_rows].add(table_grad[NODE_DEV:])
        return (graph_grad, bases_acc, coef_acc), conv_out

    start_carry = (jnp.zeros((NODES, D), jnp.float32), jnp.zeros((BASES, D, D), jnp.float32),
                   jnp.zeros((REL, BASES), jnp.float32))
    carry, conv_all = lax.scan(device_step, start_carry, jnp.arange(DEVICES, dtype=jnp.int32))
    graph_grad, bases_acc, coef_acc = carry
    layer_out = attended.reshape(NODES, D) + conv_all.reshape(NODES, D)

    grad_heads = cotangent.reshape(NODES, HEADS, HEAD_DIM)
    num_grad = grad_heads / normalizer[:, :, None]
    den_grad = -jnp.sum(grad_heads * attended, axis=2) / normalizer
    query_side = jnp.einsum('ihe,hde->ihd', num_grad, kv_sum, precision=precise) + den_grad[:, :, None] * ks_sum[None]
    dkv_sum = jnp.einsum('ihd,ihe->hde', exp_query, num_grad, precision=precise)
    dks_sum = jnp.einsum('ihd,ih->hd', exp_query, den_grad, precision=precise)
    key_side = jnp.einsum('ihe,hde->ihd', values, dkv_sum, precision=precise) + dks_sum[None]
    value_side = jnp.einsum('ihd,hde->ihe', exp_key, dkv_sum, precision=precise)
    proj_grad = jnp.concatenate([(query_side * exp_query).reshape(NODES, D), (key_side * exp_key).reshape(NODES, D),
                                 value_side.reshape(NODES, D)], axis=1).astype(jnp.bfloat16)
    grad_x = jnp.dot(proj_grad, w_all.T, preferred_element_type=jnp.float32) + graph_grad
    weight_all = jnp.dot(features.T, proj_grad, preferred_element_type=jnp.float32) * norm_scale
    query_grad = weight_all[:, :D]
    key_grad = weight_all[:, D:2 * D]
    value_grad = weight_all[:, 2 * D:]
    return (layer_out, grad_x, query_grad, key_grad, value_grad, bases_acc * norm_scale, coef_acc * norm_scale)
```

```python
import functools
import math

import jax
import jax.numpy as jnp
from jax import lax
from jax.experimental import pallas as pl
from jax.experimental.pallas import tpu as pltpu
from jax.sharding import PartitionSpec as P

HEAD_DIM = 64
TILE = 128
LANES = 128

f32 = jnp.float32
bf16 = jnp.bfloat16
NN = (((1,), (0,)), ((), ()))
NT = (((1,), (1,)), ((), ()))
TN = (((0,), (0,)), ((), ()))

VMEM = pl.BlockSpec(memory_space=pltpu.VMEM)
SMEM = pl.BlockSpec(memory_space=pltpu.SMEM)


def mm(a, b, dims=NN):
    return lax.dot_general(a, b, dims, preferred_element_type=f32)


def split(x):
    high = x.astype(bf16)
    return high, (x - high.astype(f32)).astype(bf16)


def mm_exact_right(a, b, dims=NN):
    high, low = split(a)
    return mm(high, b, dims) + mm(low, b, dims)


def mm_wide(a, b, dims=NN):
    ah, al = split(a)
    bh, bl = split(b)
    return mm(ah, bh, dims) + (mm(ah, bl, dims) + mm(al, bh, dims))


def call(body, out_shape, n_smem, n_vmem, scratch=()):
    return pl.pallas_call(
        body,
        out_shape=out_shape,
        in_specs=[SMEM] * n_smem + [VMEM] * n_vmem,
        out_specs=jax.tree.map(lambda _: VMEM, out_shape),
        scratch_shapes=list(scratch),
        compiler_params=pltpu.CompilerParams(vmem_limit_bytes=56 * 1024 * 1024),
    )


def iota(shape, dim):
    return lax.broadcasted_iota(jnp.int32, shape, dim)


def one_hot_rows(index_row, count):
    return jnp.where(iota((count, index_row.shape[1]), 0) == index_row, 1.0, 0.0).astype(bf16)


def head_mask():
    return (iota((LANES, LANES), 0) < HEAD_DIM) == (iota((LANES, LANES), 1) < HEAD_DIM)


def block_diagonal(packed):
    return jnp.where(head_mask(), jnp.concatenate([packed, packed], axis=0), 0.0)


def pack_diagonal(full):
    left = iota((HEAD_DIM, LANES), 1) < HEAD_DIM
    return jnp.where(left, full[:HEAD_DIM], full[HEAD_DIM:])


def store_summary(me, pair, pairs, packed, row, mine_ref, theirs_ref):
    half = pairs // 2
    at = (pair % half) * LANES
    side = pair // half
    tail = jnp.where(iota((8, LANES), 0) == 0, row, 0.0)

    @pl.when(me == side)
    def _():
        mine_ref[0:HEAD_DIM, at : at + LANES] = packed
        mine_ref[HEAD_DIM : HEAD_DIM + 8, at : at + LANES] = tail

    @pl.when(me != side)
    def _():
        theirs_ref[0:HEAD_DIM, at : at + LANES] = packed
        theirs_ref[HEAD_DIM : HEAD_DIM + 8, at : at + LANES] = tail


def load_summary(me, pair, pairs, mine_ref, theirs_ref):
    half = pairs // 2
    at = (pair % half) * LANES
    both = jnp.where(
        me == pair // half, mine_ref[:, at : at + LANES], theirs_ref[:, at : at + LANES]
    )
    return both[:HEAD_DIM], both[HEAD_DIM : HEAD_DIM + 1]


def gather_kernel(send_ref, features_ref, out_ref):
    pick = one_hot_rows(send_ref[...], features_ref.shape[0])
    out_ref[...] = mm(pick, features_ref[...], TN).astype(bf16)


def project_kernel(me_ref, features_ref, wq_ref, wk_ref, wv_ref, eq_ref, ek_ref, v_ref, mine_ref, theirs_ref):
    me = me_ref[0]
    features = features_ref[...]
    pairs = features.shape[1] // LANES
    ek_ref[...] = jnp.exp(mm(features, wk_ref[...]))
    v_ref[...] = mm(features, wv_ref[...])
    for p in range(pairs):
        at = slice(p * LANES, (p + 1) * LANES)
        key = ek_ref[:, at]
        full = mm_wide(key, v_ref[:, at], TN)
        store_summary(
            me, p, pairs, pack_diagonal(full), jnp.sum(key, axis=0, keepdims=True), mine_ref, theirs_ref
        )
    eq_ref[...] = jnp.exp(mm(features, wq_ref[...]))


def attend_kernel(
    me_ref, eq_ref, cot_ref, sum_mine_ref, sum_theirs_ref, att_ref, qblock_ref, mine_ref, theirs_ref
):
    me = me_ref[0]
    pairs = eq_ref.shape[1] // LANES
    same_head = jnp.where(head_mask(), 1.0, 0.0).astype(bf16)
    for p in range(pairs):
        at = slice(p * LANES, (p + 1) * LANES)
        kv, ks = load_summary(me, p, pairs, sum_mine_ref, sum_theirs_ref)
        kv = block_diagonal(kv)
        query = eq_ref[:, at]
        cot = cot_ref[:, at]
        inverse = 1.0 / mm_exact_right(query * ks, same_head)
        attended = mm_wide(query, kv) * inverse
        att_ref[:, at] = attended
        num_grad = cot * inverse
        den_grad = -mm_exact_right(cot * attended, same_head) * inverse
        full = mm_wide(query, num_grad, TN)
        row = jnp.sum(query * den_grad, axis=0, keepdims=True)
        store_summary(me, p, pairs, pack_diagonal(full), row, mine_ref, theirs_ref)
        query_side = mm_wide(num_grad, kv, NT) + den_grad * ks
        qblock_ref[:, at] = (query_side * query).astype(bf16)


def key_kernel(
    me_ref, ek_ref, v_ref, features_ref, sum_mine_ref, sum_theirs_ref, kblock_ref, vblock_ref, mine_ref, theirs_ref
):
    me = me_ref[0]
    pairs = ek_ref.shape[1] // LANES
    for p in range(pairs):
        at = slice(p * LANES, (p + 1) * LANES)
        dkv, dks = load_summary(me, p, pairs, sum_mine_ref, sum_theirs_ref)
        dkv = block_diagonal(dkv)
        key = ek_ref[:, at]
        key_side = mm_wide(v_ref[:, at], dkv, NT) + dks
        kblock_ref[:, at] = (key_side * key).astype(bf16)
        vblock_ref[:, at] = mm_wide(key, dkv).astype(bf16)
    store_halves(me, mm(features_ref[...], kblock_ref[...], TN), mine_ref, theirs_ref, slice(None))


def store_halves(me, whole, mine_ref, theirs_ref, at):
    rows = whole.shape[0] // 2
    low, high = whole[:rows], whole[rows:]
    mine_ref[:, at] = jnp.where(me == 0, low, high)
    theirs_ref[:, at] = jnp.where(me == 0, high, low).astype(bf16)


def input_grad_kernel(
    send_ref, qblock_ref, kblock_ref, vblock_ref, wq_ref, wk_ref, wv_ref, own_ref, returned_ref, out_ref
):
    total = mm(qblock_ref[...], wq_ref[...], NT) + mm(kblock_ref[...], wk_ref[...], NT)
    total += mm(vblock_ref[...], wv_ref[...], NT) + own_ref[...]
    out_ref[...] = total + mm(one_hot_rows(send_ref[...], out_ref.shape[0]), returned_ref[...])


def early_weight_kernel(me_ref, features_ref, qblock_ref, ek_ref, mine_ref, theirs_ref):
    me = me_ref[0]
    features = features_ref[...]
    width = features.shape[1]
    store_halves(me, mm(features, qblock_ref[...], TN), mine_ref, theirs_ref, slice(0, width))
    high, low = split(ek_ref[...])
    store_halves(
        me, mm(features, high, TN) + mm(features, low, TN), mine_ref, theirs_ref, slice(width, 2 * width)
    )


def incidence_kernel(count_ref, coef_ref, src_ref, dst_ref, high_ref, low_ref, hit_ref, rows_ref):
    relations, tiles, slots = src_ref.shape
    basis_count, nodes, table_rows = high_ref.shape
    for t in range(tiles):
        picks = []
        for r in range(relations):
            live = iota((TILE, slots), 1) < count_ref[r, t]
            hit = jnp.where(
                (iota((TILE, slots), 0) == dst_ref[r, t : t + 1, :]) & live, 1.0, 0.0
            )
            degree = jnp.maximum(jnp.sum(hit, axis=1, keepdims=True), 1.0)
            hit = hit / degree
            at = slice(r * slots, (r + 1) * slots)
            hit_ref[t, :, at] = hit
            for b in range(basis_count):
                rows_ref[b * TILE : (b + 1) * TILE, at] = hit * coef_ref[r, b]
            picks.append(one_hot_rows(src_ref[r, t : t + 1, :], table_rows))
        pick = jnp.concatenate(picks, axis=1)
        high, low = split(rows_ref[...])
        mixed = mm(high, pick, NT) + mm(low, pick, NT)
        high, low = split(mixed)
        for b in range(basis_count):
            high_ref[b, t * TILE : (t + 1) * TILE, :] = high[b * TILE : (b + 1) * TILE]
            low_ref[b, t * TILE : (t + 1) * TILE, :] = low[b * TILE : (b + 1) * TILE]


def convolve_kernel(
    me_ref, high_ref, low_ref, own_ref, halo_ref, bases_ref, cot_ref, conv_ref, mine_ref, theirs_ref
):
    me = me_ref[0]
    basis_count, nodes, _ = high_ref.shape
    width = own_ref.shape[1]
    cot = cot_ref[...].astype(bf16)
    own, halo = own_ref[...], halo_ref[...]
    conv = None
    for b in range(basis_count):
        basis_in = (
            mm(high_ref[b, :, :nodes], own)
            + mm(low_ref[b, :, :nodes], own)
            + mm(high_ref[b, :, nodes:], halo)
            + mm(low_ref[b, :, nodes:], halo)
        ).astype(bf16)
        part = mm(basis_in, bases_ref[b])
        conv = part if conv is None else conv + part
        store_halves(me, mm(basis_in, cot, TN), mine_ref, theirs_ref, slice(b * width, (b + 1) * width))
    conv_ref[...] = conv


def basis_grad_kernel(bases_ref, cot_ref, high_ref, low_ref, out_ref, own_ref, halo_ref):
    basis_count, nodes, _ = high_ref.shape
    cot = cot_ref[...].astype(bf16)
    total = None
    for b in range(basis_count):
        grad = mm(cot, bases_ref[b], NT)
        out_ref[b] = grad
        grad_high, grad_low = split(grad)
        part = mm(high_ref[b], grad_high, TN) + mm(high_ref[b], grad_low, TN) + mm(low_ref[b], grad_high, TN)
        total = part if total is None else total + part
    own_ref[...] = total[:nodes]
    halo_ref[...] = total[nodes:].astype(bf16)


def coef_kernel(src_ref, hit_ref, grad_ref, own_ref, halo_ref, out_ref):
    relations, tiles, slots = src_ref.shape
    basis_count, nodes, width = grad_ref.shape
    table_rows = nodes + halo_ref.shape[0]
    table = jnp.concatenate([own_ref[...], halo_ref[...]], axis=0)
    sums = jnp.zeros((basis_count, relations * slots), f32)
    for t in range(tiles):
        grads = jnp.concatenate([grad_ref[b, t * TILE : (t + 1) * TILE, :] for b in range(basis_count)], axis=0)
        high, low = split(grads)
        dots = mm(high, table, NT) + mm(low, table, NT)
        pick = jnp.concatenate([one_hot_rows(src_ref[r, t : t + 1, :], table_rows) for r in range(relations)], axis=1)
        high, low = split(dots)
        edge = mm(high, pick) + mm(low, pick)
        hit = hit_ref[t]
        sums += jnp.concatenate(
            [jnp.sum(edge[b * TILE : (b + 1) * TILE] * hit, axis=0, keepdims=True) for b in range(basis_count)], axis=0
        )
    row, lane = iota((8, LANES), 0), iota((8, LANES), 1)
    total = jnp.zeros((8, LANES), f32)
    for r in range(relations):
        part = jnp.sum(sums[:, r * slots : (r + 1) * slots], axis=1, keepdims=True)
        for b in range(basis_count):
            total = jnp.where((row == r) & (lane == b), part[b : b + 1, :], total)
    out_ref[...] = total


def add_kernel(a_ref, b_ref, out_ref):
    out_ref[...] = a_ref[...] + b_ref[...]


def finish_kernel(me_ref, mine_ref, theirs_ref, *out_refs, scale):
    me = me_ref[0]
    rows = mine_ref.shape[0]
    at = 0
    for out_ref in out_refs:
        for i in range(out_ref.shape[0]):
            width = out_ref.shape[2]
            a = mine_ref[:, at : at + width].astype(f32) * scale
            b = theirs_ref[:, at : at + width].astype(f32) * scale
            out_ref[i, :rows, :] = jnp.where(me == 0, a, b)
            out_ref[i, rows:, :] = jnp.where(me == 0, b, a)
            at += width


def value_finish_kernel(me_ref, sum_mine_ref, sum_theirs_ref, mine_ref, theirs_ref, out_ref, *, scale):
    me = me_ref[0]
    rows, width = mine_ref.shape
    pairs = width // LANES
    for p in range(pairs):
        at = slice(p * LANES, (p + 1) * LANES)
        dkv, _ = load_summary(me, p, pairs, sum_mine_ref, sum_theirs_ref)
        dkv = block_diagonal(dkv)
        a = mm_exact_left(mine_ref[:, at], dkv) * scale
        b = mm_exact_left(theirs_ref[:, at], dkv) * scale
        out_ref[:rows, at] = jnp.where(me == 0, a, b)
        out_ref[rows:, at] = jnp.where(me == 0, b, a)


def mm_exact_left(a, b, dims=NN):
    high, low = split(b)
    return mm(a, high, dims) + mm(a, low, dims)


def swap_cores(x):
    return lax.ppermute(x, "outer", [(0, 1), (1, 0)])


def all_nodes_sum(x, nodes):
    step = 1
    while step < nodes:
        x = x + lax.ppermute(x, "nodes", [(i, i ^ step) for i in range(nodes)])
        step *= 2
    return x


def reduce_wide(mine, theirs, nodes):
    rows, width = mine.shape
    half = (mine + swap_cores(theirs).astype(f32)).astype(bf16)
    parts = lax.all_to_all(
        half.reshape(nodes, rows // nodes, width), "nodes", split_axis=0, concat_axis=0, tiled=True
    )
    part = jnp.sum(parts.astype(f32), axis=0).astype(bf16)
    whole = lax.all_to_all(
        jnp.broadcast_to(part[None], parts.shape), "nodes", split_axis=0, concat_axis=0, tiled=True
    )
    return whole.reshape(rows, width)


def per_device(
    features, w_query, w_key, w_value, bases, rel_coef, send_rows, tile_src, tile_dst, tile_count, cotangent
):
    rows, width = features.shape
    nodes = lax.axis_size("nodes")
    scale = 1.0 / math.sqrt(rows * nodes * lax.axis_size("outer"))
    basis_count = bases.shape[0]
    slots = send_rows.shape[2]
    halo_rows = nodes * slots
    table_rows = rows + halo_rows
    me = lax.axis_index("outer").astype(jnp.int32).reshape(1)
    send = send_rows.reshape(1, halo_rows)
    src, dst, count = tile_src[0], tile_dst[0], tile_count[0]
    relations, tiles, cap = src.shape

    def shape(*dims, dtype=f32):
        return jax.ShapeDtypeStruct(dims, dtype)

    outgoing = call(gather_kernel, shape(halo_rows, width, dtype=bf16), 0, 2)(send, features)
    halo = lax.all_to_all(
        outgoing.reshape(nodes, slots, width), "nodes", split_axis=0, concat_axis=0, tiled=True
    ).reshape(halo_rows, width)

    summary = shape(HEAD_DIM + 8, width // 2)
    square = shape(rows, width)
    exp_query, exp_key, values, kv_mine, kv_theirs = call(
        project_kernel, (square, square, square, summary, summary), 1, 4
    )(me, features, w_query, w_key, w_value)
    kv_mine = all_nodes_sum(kv_mine + swap_cores(kv_theirs), nodes)
    kv_theirs = swap_cores(kv_mine)

    incidence = shape(basis_count, rows, table_rows, dtype=bf16)
    high, low, hits = call(
        incidence_kernel,
        (incidence, incidence, shape(tiles, TILE, relations * cap)),
        2,
        2,
        [pltpu.VMEM((basis_count * TILE, relations * cap), f32)],
    )(count, rel_coef, src, dst)

    attended, qblock, dkv_mine, dkv_theirs = call(
        attend_kernel, (square, shape(rows, width, dtype=bf16), summary, summary), 1, 4
    )(me, exp_query, cotangent, kv_mine, kv_theirs)
    dkv_mine = all_nodes_sum(dkv_mine + swap_cores(dkv_theirs), nodes)
    dkv_theirs = swap_cores(dkv_mine)

    def halves(n):
        return shape(width // 2, n * width), shape(width // 2, n * width, dtype=bf16)

    conv_out, bases_mine, bases_theirs = call(convolve_kernel, (square, *halves(basis_count)), 1, 6)(
        me, high, low, features, halo, bases, cotangent
    )
    layer_out = call(add_kernel, square, 0, 2)(attended, conv_out)
    basis_grad, own_grad, halo_grad = call(
        basis_grad_kernel, (shape(basis_count, rows, width), square, shape(halo_rows, width, dtype=bf16)), 0, 4
    )(bases, cotangent, high, low)
    returned = lax.all_to_all(
        halo_grad.reshape(nodes, slots, width), "nodes", split_axis=0, concat_axis=0, tiled=True
    ).reshape(halo_rows, width)
    bases_mine = reduce_wide(bases_mine, bases_theirs, nodes)
    bases_theirs = swap_cores(bases_mine)

    early_mine, early_theirs = call(early_weight_kernel, halves(2), 1, 3)(me, features, qblock, exp_key)
    early_mine = reduce_wide(early_mine, early_theirs, nodes)
    early_theirs = swap_cores(early_mine)

    coef_part = call(coef_kernel, shape(8, LANES), 0, 5)(src, hits, basis_grad, features, halo)
    coef_sum = coef_part + swap_cores(coef_part)
    coef_sum = all_nodes_sum(coef_sum, nodes)

    half_block = shape(rows, width, dtype=bf16)
    kblock, vblock, key_mine, key_theirs = call(key_kernel, (half_block, half_block, *halves(1)), 1, 5)(
        me, exp_key, values, features, dkv_mine, dkv_theirs
    )
    key_mine = reduce_wide(key_mine, key_theirs, nodes)
    key_theirs = swap_cores(key_mine)

    grad_x = call(input_grad_kernel, square, 0, 9)(
        send, qblock, kblock, vblock, w_query, w_key, w_value, own_grad, returned
    )

    finish = functools.partial(finish_kernel, scale=scale)
    bases_grad = call(finish, (shape(basis_count, width, width),), 1, 2)(me, bases_mine, bases_theirs)[0]
    query_grad = call(finish, (shape(1, width, width),), 1, 2)(
        me, early_mine[:, :width], early_theirs[:, :width]
    )[0][0]
    value_grad = call(functools.partial(value_finish_kernel, scale=scale), shape(width, width), 1, 4)(
        me, dkv_mine, dkv_theirs, early_mine[:, width:], early_theirs[:, width:]
    )
    key_grad = call(finish, (shape(1, width, width),), 1, 2)(me, key_mine, key_theirs)[0][0]
    coef_grad = coef_sum[:relations, :basis_count] * scale
    return layer_out, grad_x, query_grad, key_grad, value_grad, bases_grad, coef_grad


def solution(mesh):
    both = ("outer", "nodes")
    in_specs = (
        P(both, None),
        P(),
        P(),
        P(),
        P(),
        P(),
        P(both, None, None),
        P(both, None, None, None),
        P(both, None, None, None),
        P(both, None, None),
        P(both, None),
    )
    out_specs = (P(both, None), P(both, None), P(), P(), P(), P(), P())
    return jax.shard_map(per_device, mesh=mesh, in_specs=in_specs, out_specs=out_specs, check_vma=False)
```

```python
import functools
import math

import jax
import jax.numpy as jnp
from jax import lax
from jax.experimental import pallas as pl
from jax.experimental.pallas import tpu as pltpu
from jax.sharding import PartitionSpec as P

HEAD_DIM = 64
TILE = 128
LANES = 128

f32 = jnp.float32
bf16 = jnp.bfloat16
NN = (((1,), (0,)), ((), ()))
NT = (((1,), (1,)), ((), ()))
TN = (((0,), (0,)), ((), ()))

VMEM = pl.BlockSpec(memory_space=pltpu.VMEM)
SMEM = pl.BlockSpec(memory_space=pltpu.SMEM)


def shape(*dims, dtype=f32):
    return jax.ShapeDtypeStruct(dims, dtype)


def call(body, outs, scalars, arrays, after=(), megabytes=8, far=(), us=0.3):
    n_in, n_after, n_far = len(scalars) + len(arrays), len(after), len(far)

    def kernel(*refs):
        outs_at = n_in + n_after + n_far
        sources, given = refs[n_in + n_after : outs_at], refs[outs_at : outs_at + len(outs)]
        targets, sems = refs[outs_at + len(outs) : outs_at + len(outs) + n_far], refs[-1]
        moves = [pltpu.make_async_copy(sources[i], targets[i], sems.at[i]) for i in range(n_far)]
        for move in moves:
            move.start()
        for move in moves:
            move.wait()
        body(*refs[:n_in], *targets, *given)

    scratch = [pltpu.VMEM(x.shape, x.dtype) for x in far]
    return pl.pallas_call(
        kernel,
        out_shape=list(outs),
        in_specs=[SMEM] * len(scalars)
        + [VMEM] * (len(arrays) + n_after)
        + [pl.BlockSpec(memory_space=pltpu.HBM)] * n_far,
        out_specs=[VMEM] * len(outs),
        scratch_shapes=scratch + ([pltpu.SemaphoreType.DMA((n_far,))] if n_far else []),
        compiler_params=pltpu.CompilerParams(vmem_limit_bytes=megabytes * 1024 * 1024),
        cost_estimate=pl.CostEstimate(
            flops=int(us * 1.1e9),
            bytes_accessed=sum(x.size * x.dtype.itemsize for x in (*arrays, *far)),
            transcendentals=0,
        ),
    )(*scalars, *arrays, *after, *far)


def on_core_zero(place_ref):
    return place_ref[0:1, 0:1] == 0


def bit_is_zero(place_ref, bit):
    return place_ref[1 + bit : 2 + bit, 0:1] == 0


def mm(a, b, dims=NN):
    return lax.dot_general(a, b, dims, preferred_element_type=f32)


def split(x):
    high = x.astype(bf16)
    return high, (x - high.astype(f32)).astype(bf16)


def mm_exact_right(a, b, dims=NN):
    high, low = split(a)
    return mm(high, b, dims) + mm(low, b, dims)


def mm_exact_left(a, b, dims=NN):
    high, low = split(b)
    return mm(a, high, dims) + mm(a, low, dims)


def mm_wide(a, b, dims=NN):
    ah, al = split(a)
    bh, bl = split(b)
    return mm(ah, bh, dims) + (mm(ah, bl, dims) + mm(al, bh, dims))


def iota(dims, axis):
    return lax.broadcasted_iota(jnp.int32, dims, axis)


def one_hot_rows(index_row, count):
    return jnp.where(iota((count, index_row.shape[1]), 0) == index_row, 1.0, 0.0).astype(bf16)


def head_mask():
    return (iota((LANES, LANES), 0) < HEAD_DIM) == (iota((LANES, LANES), 1) < HEAD_DIM)


def block_diagonal(packed):
    return jnp.where(head_mask(), jnp.concatenate([packed, packed], axis=0), 0.0)


def pack_diagonal(full):
    left = iota((HEAD_DIM, LANES), 1) < HEAD_DIM
    return jnp.where(left, full[:HEAD_DIM], full[HEAD_DIM:])


def store_summary(place_ref, packed, rows, mine_ref, theirs_ref, extra=None):
    zero = on_core_zero(place_ref)
    half = len(packed) // 2
    first = iota((8, LANES), 0) == 0
    if extra is not None:
        at = slice(HEAD_DIM + 8, HEAD_DIM + 16)
        mine_ref[at, :] = jnp.zeros((8, mine_ref.shape[1]), f32)
        theirs_ref[at, :] = jnp.zeros((8, mine_ref.shape[1]), f32)
        mine_ref[at, :LANES] = jnp.where(zero, extra, 0.0)
        theirs_ref[at, :LANES] = jnp.where(zero, 0.0, extra)
    for p in range(half):
        at = slice(p * LANES, (p + 1) * LANES)
        low = jnp.concatenate([packed[p], jnp.where(first, rows[p], 0.0)], axis=0)
        high = jnp.concatenate([packed[p + half], jnp.where(first, rows[p + half], 0.0)], axis=0)
        mine_ref[: HEAD_DIM + 8, at] = jnp.where(zero, low, high)
        theirs_ref[: HEAD_DIM + 8, at] = jnp.where(zero, high, low)


def load_summary(place_ref, pair, pairs, mine_ref, theirs_ref):
    half = pairs // 2
    at = slice(pair % half * LANES, (pair % half + 1) * LANES)
    low, high = (mine_ref, theirs_ref) if pair < half else (theirs_ref, mine_ref)
    both = jnp.where(on_core_zero(place_ref), low[:, at], high[:, at])
    return both[:HEAD_DIM], both[HEAD_DIM : HEAD_DIM + 1]


def store_halves(place_ref, whole, mine_ref, theirs_ref, at):
    zero = on_core_zero(place_ref)
    rows = whole.shape[0] // 2
    low, high = whole[:rows], whole[rows:]
    mine_ref[:, at] = jnp.where(zero, low, high)
    theirs_ref[:, at] = jnp.where(zero, high, low).astype(bf16)


def send_row(send_ref):
    return jnp.concatenate([send_ref[p : p + 1, :] for p in range(send_ref.shape[0])], axis=1)


def gather_kernel(send_ref, features_ref, out_ref):
    pick = one_hot_rows(send_row(send_ref), features_ref.shape[0])
    out_ref[...] = mm(pick, features_ref[...], TN).astype(bf16)


def project_kernel(
    place_ref, features_ref, wk_ref, wv_ref, wq_ref, ek_ref, v_ref, eq_ref, mine_ref, theirs_ref
):
    features = features_ref[...]
    pairs = features.shape[1] // LANES
    ek_ref[...] = jnp.exp(mm(features, wk_ref[...]))
    v_ref[...] = mm(features, wv_ref[...])
    packed, sums = [], []
    for p in range(pairs):
        at = slice(p * LANES, (p + 1) * LANES)
        key = ek_ref[:, at]
        packed.append(pack_diagonal(mm_wide(key, v_ref[:, at], TN)))
        sums.append(jnp.sum(key, axis=0, keepdims=True))
    store_summary(place_ref, packed, sums, mine_ref, theirs_ref)
    eq_ref[...] = jnp.exp(mm(features, wq_ref[...]))


def attend_kernel(
    place_ref,
    eq_ref,
    cot_ref,
    sum_mine_ref,
    sum_theirs_ref,
    coef_ref,
    att_ref,
    num_ref,
    den_ref,
    mine_ref,
    theirs_ref,
):
    pairs = eq_ref.shape[1] // LANES
    same_head = jnp.where(head_mask(), 1.0, 0.0).astype(bf16)
    packed, sums = [], []
    for p in range(pairs):
        at = slice(p * LANES, (p + 1) * LANES)
        kv, ks = load_summary(place_ref, p, pairs, sum_mine_ref, sum_theirs_ref)
        kv = block_diagonal(kv)
        query = eq_ref[:, at]
        cot = cot_ref[:, at]
        inverse = 1.0 / mm_exact_right(query * ks, same_head)
        attended = mm_wide(query, kv) * inverse
        att_ref[:, at] = attended
        num_grad = cot * inverse
        den_grad = -mm_exact_right(cot * attended, same_head) * inverse
        num_ref[:, at] = num_grad
        den_ref[:, at] = den_grad
        packed.append(pack_diagonal(mm_wide(query, num_grad, TN)))
        sums.append(jnp.sum(query * den_grad, axis=0, keepdims=True))
    store_summary(place_ref, packed, sums, mine_ref, theirs_ref, coef_ref[...])


def query_kernel(
    place_ref,
    eq_ref,
    num_ref,
    den_ref,
    sum_mine_ref,
    sum_theirs_ref,
    ek_ref,
    att_ref,
    *refs,
):
    *conv_refs, features_ref, qblock_ref, layer_ref, mine_ref, theirs_ref = refs
    rows, width = eq_ref.shape
    pairs = width // LANES
    for p in range(pairs):
        at = slice(p * LANES, (p + 1) * LANES)
        kv, ks = load_summary(place_ref, p, pairs, sum_mine_ref, sum_theirs_ref)
        kv = block_diagonal(kv)
        query_side = mm_wide(num_ref[:, at], kv, NT) + den_ref[:, at] * ks
        qblock_ref[:, at] = (query_side * eq_ref[:, at]).astype(bf16)
    features = features_ref[...]
    store_halves(place_ref, mm(features, qblock_ref[...], TN), mine_ref, theirs_ref, slice(0, width))
    whole = mm_exact_left(features, ek_ref[...], TN)
    store_halves(place_ref, whole, mine_ref, theirs_ref, slice(width, 2 * width))
    for t, conv_ref in enumerate(conv_refs):
        at = slice(t * TILE, (t + 1) * TILE)
        layer_ref[at, :] = att_ref[at, :] + conv_ref[...]


def key_kernel(
    place_ref, ek_ref, v_ref, sum_mine_ref, sum_theirs_ref, features_ref, kblock_ref, mine_ref, theirs_ref
):
    pairs = ek_ref.shape[1] // LANES
    for p in range(pairs):
        at = slice(p * LANES, (p + 1) * LANES)
        dkv, dks = load_summary(place_ref, p, pairs, sum_mine_ref, sum_theirs_ref)
        key_side = mm_wide(v_ref[:, at], block_diagonal(dkv), NT) + dks
        kblock_ref[:, at] = (key_side * ek_ref[:, at]).astype(bf16)
    store_halves(place_ref, mm(features_ref[...], kblock_ref[...], TN), mine_ref, theirs_ref, slice(None))


def returned_kernel(send_ref, table_ref, returned_ref, out_ref):
    rows = out_ref.shape[0]
    out_ref[...] = table_ref[:rows, :] + mm(one_hot_rows(send_row(send_ref), rows), returned_ref[...])


def input_grad_kernel(
    place_ref,
    qblock_ref,
    kblock_ref,
    ek_ref,
    sum_mine_ref,
    sum_theirs_ref,
    graph_ref,
    wq_ref,
    wk_ref,
    wv_ref,
    out_ref,
):
    pairs = ek_ref.shape[1] // LANES
    blocks = []
    for p in range(pairs):
        at = slice(p * LANES, (p + 1) * LANES)
        dkv, _ = load_summary(place_ref, p, pairs, sum_mine_ref, sum_theirs_ref)
        blocks.append(mm_wide(ek_ref[:, at], block_diagonal(dkv)).astype(bf16))
    total = mm(qblock_ref[...], wq_ref[...], NT) + mm(kblock_ref[...], wk_ref[...], NT)
    out_ref[...] = total + mm(jnp.concatenate(blocks, axis=1), wv_ref[...], NT) + graph_ref[...]


def tile_hits(count_ref, dst_ref, r, tile):
    slots = dst_ref.shape[2]
    live = iota((TILE, slots), 1) < count_ref[r, tile]
    target = iota((TILE, slots), 0) == dst_ref[r, tile : tile + 1, :]
    hit = jnp.where(target & live, 1.0, 0.0)
    return hit / jnp.maximum(jnp.sum(hit, axis=1, keepdims=True), 1.0)


def tile_incidence(count_ref, coef_ref, dst_ref, tile):
    basis_count = coef_ref.shape[1]
    hits, scaled = [], [[] for _ in range(basis_count)]
    for r in range(dst_ref.shape[0]):
        hit = tile_hits(count_ref, dst_ref, r, tile)
        hits.append(hit)
        for b in range(basis_count):
            scaled[b].append(hit * coef_ref[r, b])
    high, low = split(jnp.concatenate([jnp.concatenate(part, axis=1) for part in scaled], axis=0))
    return jnp.concatenate(hits, axis=1), jnp.concatenate([high, low], axis=0)


def backward_kernel(count_ref, coef_ref, src_ref, dst_ref, grad_ref, *refs, tile):
    table_ref = refs[-1]
    _, scaled = tile_incidence(count_ref, coef_ref, dst_ref, tile)
    picks = [one_hot_rows(src_ref[r, tile : tile + 1, :], table_ref.shape[0]) for r in range(src_ref.shape[0])]
    grad = grad_ref[tile].astype(bf16)
    moved = mm(scaled, jnp.concatenate([grad, grad], axis=0), TN).astype(bf16)
    table = mm(jnp.concatenate(picks, axis=1), moved)
    table_ref[...] = table if tile == 0 else table + refs[0][...]


def one_hot_columns(index_row, count):
    lanes = index_row.shape[1]
    column = jnp.broadcast_to(index_row.astype(f32), (LANES, lanes)).T.astype(jnp.int32)
    blocks = [jnp.where(iota((lanes, LANES), 1) + j == column, 1.0, 0.0) for j in range(0, count, LANES)]
    return jnp.concatenate(blocks, axis=1).astype(bf16)


def forward_kernel(count_ref, coef_ref, src_ref, dst_ref, grad_ref, own_ref, halo_ref, bases_ref, *refs, tile, last):
    basis_ref, conv_ref, sums_ref = refs[-3:]
    relations, _, slots = src_ref.shape
    basis_count = bases_ref.shape[0]
    wide = basis_count * TILE
    rows, halo_rows = own_ref.shape[0], halo_ref.shape[0]
    hit, scaled = tile_incidence(count_ref, coef_ref, dst_ref, tile)
    picks = [one_hot_columns(src_ref[r, tile : tile + 1, :], rows + halo_rows) for r in range(relations)]
    pick = jnp.concatenate(picks, axis=0)
    edge_rows = (mm(pick[:, :rows], own_ref[...]) + mm(pick[:, rows:], halo_ref[...])).astype(bf16)
    both = mm(scaled, edge_rows)
    both = (both[:wide] + both[wide:]).astype(bf16)
    conv = None
    for b in range(basis_count):
        basis_in = both[b * TILE : (b + 1) * TILE]
        basis_ref[b] = basis_in
        part = mm(basis_in, bases_ref[b])
        conv = part if conv is None else conv + part
    conv_ref[...] = conv

    dots = mm(jnp.concatenate(split(grad_ref[tile]), axis=0), edge_rows, NT)
    dots = dots[:wide] + dots[wide:]
    row, lane = iota((8, LANES), 0), iota((8, LANES), 1)
    total = jnp.zeros((8, LANES), f32)
    for b in range(basis_count):
        sums = jnp.sum(dots[b * TILE : (b + 1) * TILE] * hit, axis=0, keepdims=True)
        if tile > 0:
            sums += refs[0][b : b + 1, :]
        if not last:
            sums_ref[b : b + 1, :] = sums
            continue
        for r in range(relations):
            part = jnp.sum(sums[:, r * slots : (r + 1) * slots], axis=1, keepdims=True)
            total = jnp.where((row == r) & (lane == b), part, total)
    if last:
        sums_ref[...] = total


def ship_kernel(table_ref, out_ref):
    out_ref[...] = table_ref[table_ref.shape[0] - out_ref.shape[0] :, :].astype(bf16)


def bases_kernel(place_ref, *refs, parts, basis_count):
    cot_ref, mine_ref, theirs_ref = refs[parts:]
    width = cot_ref.shape[1]
    cot = cot_ref[...].astype(bf16)
    for b in range(basis_count):
        basis_in = jnp.concatenate([refs[i][b] for i in range(parts)], axis=0)
        at = slice(b * width, (b + 1) * width)
        store_halves(place_ref, mm(basis_in, cot, TN), mine_ref, theirs_ref, at)


def basis_grad_kernel(bases_ref, cot_ref, out_ref, *, tiles):
    cot = cot_ref[...].astype(bf16)
    for b in range(bases_ref.shape[0]):
        grad = mm(cot, bases_ref[b], NT)
        for t in range(tiles):
            out_ref[t, b * TILE : (b + 1) * TILE, :] = grad[t * TILE : (t + 1) * TILE]


def add_kernel(a_ref, b_ref, out_ref):
    out_ref[...] = a_ref[...] + b_ref[...]


def choose(place_ref, first_bit, blocks, index):
    bit = first_bit
    while len(blocks) > 1:
        zero = bit_is_zero(place_ref, bit)
        pairs = [(blocks[i], blocks[i + 1]) for i in range(0, len(blocks), 2)]
        if index % 2:
            blocks = [jnp.where(zero, high, low) for low, high in pairs]
        else:
            blocks = [jnp.where(zero, low, high) for low, high in pairs]
        index //= 2
        bit += 1
    return blocks[0]


def scatter_kernel(place_ref, *refs, first_bit, sources):
    keep_ref, *send_refs = refs[sum(sources) :]
    rows = keep_ref.shape[0]
    count = len(send_refs) + 1
    at = 0
    for n in sources:
        parts, refs = refs[:n], refs[n:]
        width = parts[0].shape[1]
        blocks = []
        for i in range(count):
            rows_at = slice(i * rows, (i + 1) * rows)
            total = parts[0][rows_at, :].astype(f32)
            for part in parts[1:]:
                total += part[rows_at, :].astype(f32)
            blocks.append(total)
        lanes = slice(at, at + width)
        keep_ref[:, lanes] = choose(place_ref, first_bit, blocks, 0)
        for k in range(1, count):
            send_refs[k - 1][:, lanes] = choose(place_ref, first_bit, blocks, k).astype(send_refs[k - 1].dtype)
        at += width


def total_kernel(*refs):
    out_ref = refs[-1]
    total = refs[0][...].astype(f32)
    for ref in refs[1:-1]:
        total += ref[...].astype(f32)
    out_ref[...] = total.astype(out_ref.dtype)


def join_kernel(place_ref, *refs, first_bit):
    out_ref = refs[-1]
    blocks = [ref[...] for ref in refs[:-1]]
    rows = blocks[0].shape[0]
    for i in range(len(blocks)):
        out_ref[i * rows : (i + 1) * rows, :] = choose(place_ref, first_bit, blocks, i)


def finish_kernel(place_ref, sum_mine_ref, sum_theirs_ref, mine_ref, theirs_ref, *refs, scale, basis_count):
    bases_ref, *outs = refs[:4]
    outs = [bases_ref.at[b] for b in range(basis_count)] + outs
    holds, sems = refs[4:-1], refs[-1]
    zero = on_core_zero(place_ref)
    rows = mine_ref.shape[0]
    width = holds[0].shape[1]
    moves = []
    for i, hold in enumerate(holds):
        for p in range(width // LANES):
            at = slice(p * LANES, (p + 1) * LANES)
            source = slice(i * width + p * LANES, i * width + (p + 1) * LANES)
            if i == basis_count + 1:
                dkv, _ = load_summary(place_ref, p, width // LANES, sum_mine_ref, sum_theirs_ref)
                dkv = block_diagonal(dkv)
                a = mm_exact_left(mine_ref[:, source], dkv) * scale
                b = mm_exact_left(theirs_ref[:, source], dkv) * scale
            else:
                a = mine_ref[:, source].astype(f32) * scale
                b = theirs_ref[:, source].astype(f32) * scale
            hold[:rows, at] = jnp.where(zero, a, b)
            hold[rows:, at] = jnp.where(zero, b, a)
        moves.append(pltpu.make_async_copy(hold, outs[i], sems.at[i]))
        moves[-1].start()
    for move in moves:
        move.wait()


def swap_cores(x):
    return lax.ppermute(x, "outer", [(0, 1), (1, 0)])


def swap_nodes(x, bit):
    nodes = lax.axis_size("nodes")
    return lax.ppermute(x, "nodes", [(i, i ^ (1 << bit)) for i in range(nodes)])


def sum_summary(mine, theirs, bits, beside):
    out = [shape(*mine.shape)]
    received = swap_cores(theirs)
    (mine,) = call(add_kernel, out, [], [mine, received], beside("core", mine))
    for bit in bits:
        received = swap_nodes(mine, bit)
        (mine,) = call(add_kernel, out, [], [mine, received], beside(bit, mine))
    return mine, swap_cores(mine), beside("back", mine)


def exchange(sends, first_bit):
    nodes = lax.axis_size("nodes")
    return [
        lax.ppermute(x, "nodes", [(i, i ^ (k << first_bit)) for i in range(nodes)])
        for k, x in enumerate(sends, start=1)
    ]


def per_device(
    features, w_query, w_key, w_value, bases, rel_coef, send_rows, tile_src, tile_dst, tile_count, cotangent
):
    rows, width = features.shape
    nodes = lax.axis_size("nodes")
    scale = 1.0 / math.sqrt(rows * nodes * lax.axis_size("outer"))
    basis_count = bases.shape[0]
    slots = send_rows.shape[2]
    halo_rows = nodes * slots
    table_rows = rows + halo_rows
    core, node = lax.axis_index("outer"), lax.axis_index("nodes")
    place = jnp.stack([core] + [(node >> bit) & 1 for bit in range(7)]).astype(jnp.int32)
    place = jnp.broadcast_to(place[:, None], (8, LANES))
    send, src, dst, count = send_rows[0], tile_src[0], tile_dst[0], tile_count[0]
    relations, tiles, cap = src.shape
    bits = list(range(nodes.bit_length() - 1))
    y, z1, z2 = bits[-3:]

    square, square_half = shape(rows, width), shape(rows, width, dtype=bf16)
    summary = shape(HEAD_DIM + 8, width // 2)
    wide_summary = shape(HEAD_DIM + 16, width // 2)

    def halves(n):
        return shape(width // 2, n * width), shape(width // 2, n * width, dtype=bf16)

    (outgoing,) = call(gather_kernel, [shape(halo_rows, width, dtype=bf16)], [], [send], far=[features], us=1.4)
    halo = lax.all_to_all(
        outgoing.reshape(nodes, slots, width), "nodes", split_axis=0, concat_axis=0, tiled=True
    ).reshape(halo_rows, width)
    exp_key, values, exp_query, kv_mine, kv_theirs = call(
        project_kernel,
        [square, square, square, summary, summary],
        [],
        [place],
        far=[features, w_key, w_value, w_query],
        us=1.8,
    )

    kept = {}

    def run_basis_grad(x):
        (kept["grad"],) = call(
            functools.partial(basis_grad_kernel, tiles=tiles),
            [shape(tiles, basis_count * TILE, width)],
            [],
            [],
            [x],
            far=[bases, cotangent],
            us=1.1,
        )
        return kept["grad"]

    def run_backward(t, x):
        (kept["table"],) = call(
            functools.partial(backward_kernel, tile=t),
            [shape(table_rows, width)],
            [count, rel_coef],
            [src, dst, kept["grad"]] + ([kept["table"]] if t > 0 else []),
            [x],
            table_rows // 64,
            us=2.7,
        )
        return kept["table"]

    def run_forward(t, x):
        last = t == tiles - 1
        outs = [shape(basis_count, TILE, width, dtype=bf16), shape(TILE, width)]
        outs.append(shape(8, LANES) if last else shape(8, relations * cap))
        kept["basis", t], kept["conv", t], kept["coef"] = call(
            functools.partial(forward_kernel, tile=t, last=last),
            outs,
            [count, rel_coef],
            [src, dst, kept["grad"], features, halo, bases] + ([kept["coef"]] if t > 0 else []),
            [x],
            table_rows // 64,
            us=3.3,
        )
        return kept["coef"]

    def run_bases(x):
        kept["bases"] = call(
            functools.partial(bases_kernel, parts=tiles, basis_count=basis_count),
            halves(basis_count),
            [],
            [place, *[kept["basis", t] for t in range(tiles)], cotangent],
            [x],
            us=0.8,
        )
        return kept["bases"][1]

    def run_ship(x):
        (sent,) = call(ship_kernel, [shape(halo_rows, width, dtype=bf16)], [], [kept["table"]], [x])
        kept["returned"] = lax.all_to_all(
            sent.reshape(nodes, slots, width), "nodes", split_axis=0, concat_axis=0, tiled=True
        ).reshape(halo_rows, width)
        return sent

    backward = [functools.partial(run_backward, t) for t in range(tiles)]
    forward = [functools.partial(run_forward, t) for t in range(tiles)]
    first = {"core": [run_basis_grad], bits[0]: backward[:1], y: backward[1:2], z1: backward[2:3], z2: backward[3:]}
    first["back"] = [run_ship, *forward, run_bases]
    kv_mine, kv_theirs, after = sum_summary(
        kv_mine, kv_theirs, bits, lambda step, x: [run(x) for run in first.get(step, [])]
    )
    attended, num_grad, den_grad, dkv_mine, dkv_theirs = call(
        attend_kernel,
        [square, square, square, wide_summary, wide_summary],
        [],
        [place, exp_query, cotangent, kv_mine, kv_theirs, kept["coef"]],
        after,
        us=2.0,
    )

    plane, planes = nodes // 4, 4
    plane_rows = width // 2 // plane
    place_rows = plane_rows // planes
    early_width, whole_width = (basis_count + 2) * width, (basis_count + 3) * width

    def sends(n, rows, columns):
        return [shape(rows, columns)] + [shape(rows, columns, dtype=bf16 if rows >= 16 else f32)] * (n - 1)

    def run_returned(x):
        (kept["graph"],) = call(
            returned_kernel, [square], [], [send, kept["table"], kept["returned"]], [x], us=0.5
        )
        return kept["graph"]

    def run_query(x):
        operands = [exp_query, num_grad, den_grad, kv_mine, kv_theirs, exp_key, attended]
        operands += [kept["conv", t] for t in range(tiles)]
        kept["qblock"], kept["layer"], *kept["early"] = call(
            query_kernel,
            [square_half, square, *halves(2)],
            [],
            [place, *operands],
            [x],
            12,
            far=[features],
            us=2.7,
        )
        return kept["early"][1]

    def run_early(x):
        operands = []
        for mine, theirs in (kept["bases"], kept["early"]):
            operands += [mine, swap_cores(theirs)]
        kept["early own"], *out = call(
            functools.partial(scatter_kernel, first_bit=0, sources=[2, 2]),
            sends(plane, plane_rows, early_width),
            [],
            [place, *operands],
            [x],
            12,
        )
        kept["early received"] = exchange(out, 0)
        return kept["early own"]

    def run_early_sum(x):
        (kept["early own"],) = call(
            total_kernel,
            [shape(plane_rows, early_width)],
            [],
            [kept["early own"], *kept["early received"]],
            [x],
        )
        return kept["early own"]

    second = {"core": [run_query], bits[0]: [run_returned], y: [run_early], "back": [run_early_sum]}
    dkv_mine, dkv_theirs, after = sum_summary(
        dkv_mine, dkv_theirs, bits, lambda step, x: [run(x) for run in second.get(step, [])]
    )
    kblock, key_mine, key_theirs = call(
        key_kernel,
        [square_half, *halves(1)],
        [],
        [place, exp_key, values, dkv_mine, dkv_theirs],
        after,
        far=[features],
        us=1.1,
    )
    key_own, *out = call(
        functools.partial(scatter_kernel, first_bit=0, sources=[2]),
        sends(plane, plane_rows, width),
        [],
        [place, key_mine, swap_cores(key_theirs)],
    )
    received = exchange(out, 0)
    (grad_x,) = call(
        input_grad_kernel,
        [square],
        [],
        [place, kept["qblock"], kblock, exp_key, dkv_mine, dkv_theirs, kept["graph"]],
        [key_own],
        16,
        far=[w_query, w_key, w_value],
        us=3.5,
    )
    own, *out = call(
        functools.partial(scatter_kernel, first_bit=z1, sources=[1, plane]),
        sends(planes, place_rows, whole_width),
        [],
        [place, kept["early own"], key_own, *received],
    )
    total_type = bf16 if place_rows >= 16 else f32
    (own,) = call(
        total_kernel, [shape(place_rows, whole_width, dtype=total_type)], [], [own, *exchange(out, z1)]
    )
    (own,) = call(
        functools.partial(join_kernel, first_bit=z1),
        [shape(plane_rows, whole_width, dtype=total_type)],
        [],
        [place, own, *exchange([own] * (planes - 1), z1)],
    )
    own = own.astype(bf16)
    (own,) = call(
        functools.partial(join_kernel, first_bit=0),
        [shape(width // 2, whole_width, dtype=bf16)],
        [],
        [place, own, *exchange([own] * (plane - 1), 0)],
    )
    count_out = basis_count + 3
    bases_grad, query_grad, value_grad, key_grad = pl.pallas_call(
        functools.partial(finish_kernel, scale=scale, basis_count=basis_count),
        out_shape=[shape(basis_count, width, width)] + [shape(width, width)] * 3,
        in_specs=[VMEM] * 5,
        out_specs=[pl.BlockSpec(memory_space=pltpu.HBM)] * 4,
        scratch_shapes=[pltpu.VMEM((width, width), f32)] * count_out + [pltpu.SemaphoreType.DMA((count_out,))],
        compiler_params=pltpu.CompilerParams(vmem_limit_bytes=16 * 1024 * 1024),
    )(place, dkv_mine, dkv_theirs, own, swap_cores(own))
    coef_sum = jnp.where(core == 0, dkv_mine, dkv_theirs)[HEAD_DIM + 8 :, :]
    coef_grad = coef_sum[:relations, :basis_count] * scale
    return kept["layer"], grad_x, query_grad, key_grad, value_grad, bases_grad, coef_grad


def solution(mesh):
    both = ("outer", "nodes")
    in_specs = (
        P(both, None),
        P(),
        P(),
        P(),
        P(),
        P(),
        P(both, None, None),
        P(both, None, None, None),
        P(both, None, None, None),
        P(both, None, None),
        P(both, None),
    )
    out_specs = (P(both, None), P(both, None), P(), P(), P(), P(), P())
    return jax.shard_map(per_device, mesh=mesh, in_specs=in_specs, out_specs=out_specs, check_vma=False)
```

```python
import functools
import math

import jax
import jax.numpy as jnp
from jax import lax
from jax.experimental import pallas as pl
from jax.experimental.pallas import tpu as pltpu
from jax.sharding import PartitionSpec as P

HEAD_DIM = 64
TILE = 128
LANES = 128

f32 = jnp.float32
bf16 = jnp.bfloat16
NN = (((1,), (0,)), ((), ()))
NT = (((1,), (1,)), ((), ()))
TN = (((0,), (0,)), ((), ()))

VMEM = pl.BlockSpec(memory_space=pltpu.VMEM)
HBM = pl.BlockSpec(memory_space=pltpu.HBM)


def shape(*dims, dtype=f32):
    return jax.ShapeDtypeStruct(dims, dtype)


def call(body, outs, arrays, after=(), megabytes=8, far=(), us=0.3, lazy=False, scratch=(), far_outs=()):
    n_in, n_after, n_far = len(arrays), len(after), len(far)
    n_outs, n_leave = len(outs), len(far_outs)

    def kernel(*refs):
        refs = list(refs)

        def take(n):
            taken = refs[:n]
            del refs[:n]
            return taken

        given, _, sources, results, leaving = take(n_in), take(n_after), take(n_far), take(n_outs), take(n_leave)
        targets, held, more = take(n_far), take(n_leave), take(len(scratch))
        moves = [pltpu.make_async_copy(sources[i], targets[i], refs[0].at[i]) for i in range(n_far)]
        leaves = [pltpu.make_async_copy(held[i], leaving[i], refs[0].at[n_far + i]) for i in range(n_leave)]
        for move in moves:
            move.start()
        options = {}
        if lazy:
            options["arrive"] = lambda i: moves[i].wait()
        else:
            for move in moves:
                move.wait()
        if far_outs:
            options["leave"] = lambda i: leaves[i].start()
        body(*given, *targets, *results, *held, *more, **options)
        for leave in leaves:
            leave.wait()

    scratches = [pltpu.VMEM(x.shape, x.dtype) for x in (*far, *far_outs, *scratch)]
    sems = n_far + n_leave
    return pl.pallas_call(
        kernel,
        out_shape=list(outs) + [pltpu.HBM(x.shape, x.dtype) for x in far_outs],
        in_specs=[VMEM] * (n_in + n_after) + [HBM] * n_far,
        out_specs=[VMEM] * n_outs + [HBM] * n_leave,
        scratch_shapes=scratches + ([pltpu.SemaphoreType.DMA((sems,))] if sems else []),
        compiler_params=pltpu.CompilerParams(vmem_limit_bytes=megabytes * 1024 * 1024),
        cost_estimate=pl.CostEstimate(
            flops=int(us * 1.1e9),
            bytes_accessed=sum(x.size * x.dtype.itemsize for x in arrays),
            transcendentals=0,
        ),
    )(*arrays, *after, *[pltpu.with_memory_space_constraint(x, pltpu.HBM) for x in far])


def on_core_zero(place_ref):
    return place_ref[0:1, 0:1] == 0


def bit_is_zero(place_ref, bit):
    return place_ref[1 + bit : 2 + bit, 0:1] == 0


def mm(a, b, dims=NN):
    return lax.dot_general(a, b, dims, preferred_element_type=f32)


def split(x):
    high = x.astype(bf16)
    return high, (x - high.astype(f32)).astype(bf16)


def mm_exact_right(a, b, dims=NN):
    high, low = split(a)
    return mm(high, b, dims) + mm(low, b, dims)


def mm_exact_left(a, b, dims=NN):
    high, low = split(b)
    return mm(a, high, dims) + mm(a, low, dims)


def mm_wide(a, b, dims=NN):
    ah, al = split(a)
    bh, bl = split(b)
    return mm(ah, bh, dims) + (mm(ah, bl, dims) + mm(al, bh, dims))


def iota(dims, axis):
    return lax.broadcasted_iota(jnp.int32, dims, axis)


def one_hot_rows(index_row, count):
    return jnp.where(iota((count, index_row.shape[1]), 0) == index_row, 1.0, 0.0).astype(bf16)


def head_mask():
    return (iota((LANES, LANES), 0) < HEAD_DIM) == (iota((LANES, LANES), 1) < HEAD_DIM)


def block_diagonal(packed):
    return jnp.where(head_mask(), jnp.concatenate([packed, packed], axis=0), 0.0)


def pack_diagonal(full):
    left = iota((HEAD_DIM, LANES), 1) < HEAD_DIM
    return jnp.where(left, full[:HEAD_DIM], full[HEAD_DIM:])


def store_summary(place_ref, packed, rows, mine_ref, theirs_ref, extra=None):
    zero = on_core_zero(place_ref)
    half = len(packed) // 2
    first = iota((8, LANES), 0) == 0
    if extra is not None:
        at = slice(HEAD_DIM + 8, HEAD_DIM + 16)
        mine_ref[at, :] = jnp.zeros((8, mine_ref.shape[1]), f32)
        theirs_ref[at, :] = jnp.zeros((8, mine_ref.shape[1]), f32)
        mine_ref[at, :LANES] = jnp.where(zero, extra, 0.0)
        theirs_ref[at, :LANES] = jnp.where(zero, 0.0, extra)
    for p in range(half):
        at = slice(p * LANES, (p + 1) * LANES)
        low = jnp.concatenate([packed[p], jnp.where(first, rows[p], 0.0)], axis=0)
        high = jnp.concatenate([packed[p + half], jnp.where(first, rows[p + half], 0.0)], axis=0)
        mine_ref[: HEAD_DIM + 8, at] = jnp.where(zero, low, high)
        theirs_ref[: HEAD_DIM + 8, at] = jnp.where(zero, high, low)


def load_summary(place_ref, pair, pairs, mine_ref, theirs_ref):
    half = pairs // 2
    at = slice(pair % half * LANES, (pair % half + 1) * LANES)
    low, high = (mine_ref, theirs_ref) if pair < half else (theirs_ref, mine_ref)
    both = jnp.where(on_core_zero(place_ref), low[:, at], high[:, at])
    return both[:HEAD_DIM], both[HEAD_DIM : HEAD_DIM + 1]


def store_halves(place_ref, whole, mine_ref, theirs_ref, at):
    zero = on_core_zero(place_ref)
    rows = whole.shape[0] // 2
    low, high = whole[:rows], whole[rows:]
    mine_ref[:, at] = jnp.where(zero, low, high)
    theirs_ref[:, at] = jnp.where(zero, high, low).astype(bf16)


def send_row(send_ref):
    return jnp.concatenate([send_ref[p : p + 1, :] for p in range(send_ref.shape[0])], axis=1)


def start_kernel(
    place_ref,
    features_ref,
    wq_ref,
    wk_ref,
    wv_ref,
    send_ref,
    bases_ref,
    cot_ref,
    mine_ref,
    theirs_ref,
    out_ref,
    high_ref,
    low_ref,
    eq_ref,
    ek_ref,
    v_ref,
    *,
    arrive,
    leave,
):
    pairs = features_ref.shape[1] // LANES
    arrive(0)
    features = features_ref[...]
    arrive(1)
    eq_ref[...] = jnp.exp(mm(features, wq_ref[...]))
    leave(0)
    arrive(2)
    ek_ref[...] = jnp.exp(mm(features, wk_ref[...]))
    leave(1)
    arrive(3)
    v_ref[...] = mm(features, wv_ref[...])
    leave(2)
    packed, sums = [], []
    for p in range(pairs):
        at = slice(p * LANES, (p + 1) * LANES)
        key = ek_ref[:, at]
        packed.append(pack_diagonal(mm_wide(key, v_ref[:, at], TN)))
        sums.append(jnp.sum(key, axis=0, keepdims=True))
    store_summary(place_ref, packed, sums, mine_ref, theirs_ref)
    arrive(4)
    pick = one_hot_rows(send_row(send_ref), features.shape[0])
    out_ref[...] = mm(pick, features, TN).astype(bf16)
    arrive(5)
    arrive(6)
    cot = cot_ref[...].astype(bf16)
    for b in range(bases_ref.shape[0]):
        high, low = split(mm(cot, bases_ref[b], NT))
        for t in range(high_ref.shape[0]):
            high_ref[t, b * TILE : (b + 1) * TILE, :] = high[t * TILE : (t + 1) * TILE]
            low_ref[t, b * TILE : (b + 1) * TILE, :] = low[t * TILE : (t + 1) * TILE]


def attend_kernel(
    place_ref,
    eq_ref,
    cot_ref,
    sum_mine_ref,
    sum_theirs_ref,
    coef_ref,
    conv_ref,
    mine_ref,
    theirs_ref,
    qblock_ref,
    layer_ref,
    *,
    leave,
):
    pairs = eq_ref.shape[1] // LANES
    same_head = jnp.where(head_mask(), 1.0, 0.0).astype(bf16)
    packed, sums = [], []
    for p in range(pairs):
        at = slice(p * LANES, (p + 1) * LANES)
        kv, ks = load_summary(place_ref, p, pairs, sum_mine_ref, sum_theirs_ref)
        kv = block_diagonal(kv)
        query = eq_ref[:, at]
        cot = cot_ref[:, at]
        inverse = 1.0 / mm_exact_right(query * ks, same_head)
        attended = mm_wide(query, kv) * inverse
        layer_ref[:, at] = attended + conv_ref[:, at]
        num_grad = cot * inverse
        den_grad = -mm_exact_right(cot * attended, same_head) * inverse
        packed.append(pack_diagonal(mm_wide(query, num_grad, TN)))
        sums.append(jnp.sum(query * den_grad, axis=0, keepdims=True))
        query_side = mm_wide(num_grad, kv, NT) + den_grad * ks
        qblock_ref[:, at] = (query_side * query).astype(bf16)
    leave(0)
    store_summary(place_ref, packed, sums, mine_ref, theirs_ref, coef_ref[...])


def query_kernel(place_ref, qblock_ref, ek_ref, bases_theirs_ref, features_ref, mine_ref, theirs_ref):
    width = features_ref.shape[1]
    bases_width = bases_theirs_ref.shape[1]
    theirs_ref[:, :bases_width] = bases_theirs_ref[...]
    theirs_ref = theirs_ref.at[:, bases_width:]
    features = features_ref[...]
    store_halves(place_ref, mm(features, qblock_ref[...], TN), mine_ref, theirs_ref, slice(0, width))
    whole = mm_exact_left(features, ek_ref[...], TN)
    store_halves(place_ref, whole, mine_ref, theirs_ref, slice(width, 2 * width))


def key_kernel(
    place_ref, ek_ref, v_ref, sum_mine_ref, sum_theirs_ref, features_ref, kblock_ref, mine_ref, theirs_ref
):
    pairs = ek_ref.shape[1] // LANES
    for p in range(pairs):
        at = slice(p * LANES, (p + 1) * LANES)
        dkv, dks = load_summary(place_ref, p, pairs, sum_mine_ref, sum_theirs_ref)
        key_side = mm_wide(v_ref[:, at], block_diagonal(dkv), NT) + dks
        kblock_ref[:, at] = (key_side * ek_ref[:, at]).astype(bf16)
    store_halves(place_ref, mm(features_ref[...], kblock_ref[...], TN), mine_ref, theirs_ref, slice(None))


def returned_kernel(send_ref, table_ref, returned_ref, out_ref):
    rows = out_ref.shape[0]
    out_ref[...] = table_ref[:rows, :] + mm(one_hot_rows(send_row(send_ref), rows), returned_ref[...])


def input_grad_kernel(
    place_ref,
    qblock_ref,
    kblock_ref,
    ek_ref,
    sum_mine_ref,
    sum_theirs_ref,
    graph_ref,
    wq_ref,
    wk_ref,
    wv_ref,
    out_ref,
    token_ref,
):
    token_ref[...] = jnp.zeros((8, LANES), f32)
    pairs = ek_ref.shape[1] // LANES
    blocks = []
    for p in range(pairs):
        at = slice(p * LANES, (p + 1) * LANES)
        dkv, _ = load_summary(place_ref, p, pairs, sum_mine_ref, sum_theirs_ref)
        blocks.append(mm_wide(ek_ref[:, at], block_diagonal(dkv)).astype(bf16))
    total = mm(qblock_ref[...], wq_ref[...], NT) + mm(kblock_ref[...], wk_ref[...], NT)
    out_ref[...] = total + mm(jnp.concatenate(blocks, axis=1), wv_ref[...], NT) + graph_ref[...]


def tile_hits(count_ref, dst_ref, r, tile):
    slots = dst_ref.shape[2]
    live = iota((TILE, slots), 1) < count_ref[r : r + 1, tile : tile + 1]
    target = iota((TILE, slots), 0) == dst_ref[r, tile : tile + 1, :]
    hit = jnp.where(target & live, 1.0, 0.0)
    return hit / jnp.maximum(jnp.sum(hit, axis=1, keepdims=True), 1.0)


def tile_incidence(count_ref, coef_ref, dst_ref, tile):
    basis_count = coef_ref.shape[1]
    hits, scaled = [], [[] for _ in range(basis_count)]
    for r in range(dst_ref.shape[0]):
        hit = tile_hits(count_ref, dst_ref, r, tile)
        hits.append(hit)
        for b in range(basis_count):
            scaled[b].append(hit * coef_ref[r : r + 1, b : b + 1])
    high, low = split(jnp.concatenate([jnp.concatenate(part, axis=1) for part in scaled], axis=0))
    return jnp.concatenate(hits, axis=1), jnp.concatenate([high, low], axis=0)


def tile_pick(src_ref, tile, table_rows):
    picks = [one_hot_rows(src_ref[r, tile : tile + 1, :], table_rows) for r in range(src_ref.shape[0])]
    return jnp.concatenate(picks, axis=1)


def backward_kernel(count_ref, coef_ref, src_ref, dst_ref, grad_ref, *refs, tile, last, leave):
    mixed_ref = refs[-1]
    table_ref = refs[0 if tile == 0 else 1]
    _, scaled = tile_incidence(count_ref, coef_ref, dst_ref, tile)
    both = mm(scaled, tile_pick(src_ref, tile, table_ref.shape[0]), NT)
    wide = both.shape[0] // 2
    high, low = split(both[:wide] + both[wide:])
    mixed_ref[:wide, :] = high
    mixed_ref[wide:, :] = low
    leave(0)
    table = mm(high, grad_ref[tile], TN)
    table = table if tile == 0 else table + refs[0][...]
    table_ref[...] = table
    if last:
        sent_ref = refs[-2]
        sent_ref[...] = table[table.shape[0] - sent_ref.shape[0] :, :].astype(bf16)


def forward_kernel(count_ref, coef_ref, place_ref, src_ref, dst_ref, *refs, arrive):
    relations, tiles, slots = src_ref.shape
    own_ref, halo_ref, high_ref, low_ref, bases_ref = refs[:5]
    mixed_refs, (cot_ref, conv_ref, coef_grad_ref, mine_ref, theirs_ref, basis_ref) = refs[5 : 5 + tiles], refs[5 + tiles :]
    basis_count = bases_ref.shape[0]
    wide = basis_count * TILE
    rows, width = own_ref.shape
    sums = [jnp.zeros((1, relations * slots), f32) for _ in range(basis_count)]
    for t in range(tiles):
        hit, _ = tile_incidence(count_ref, coef_ref, dst_ref, t)
        pick = tile_pick(src_ref, t, rows + halo_ref.shape[0])
        if t == 0:
            for i in range(4):
                arrive(i)
        grads = jnp.concatenate([high_ref[t], low_ref[t]], axis=0)
        dots = [mm(grads, table_ref[...], NT) for table_ref in (own_ref, halo_ref)]
        dots = [(x[:wide] + x[wide:]).astype(bf16) for x in dots]
        edge = mm(dots[0], pick[:rows]) + mm(dots[1], pick[rows:])
        for b in range(basis_count):
            sums[b] += jnp.sum(edge[b * TILE : (b + 1) * TILE] * hit, axis=0, keepdims=True)
        if t == 0:
            arrive(4)
        arrive(5 + t)
        mixed_ref = mixed_refs[t]
        both = mm(mixed_ref[:, :rows], own_ref[...]) + mm(mixed_ref[:, rows:], halo_ref[...])
        both = (both[:wide] + both[wide:]).astype(bf16)
        at = slice(t * TILE, (t + 1) * TILE)
        conv = None
        for b in range(basis_count):
            basis_in = both[b * TILE : (b + 1) * TILE]
            basis_ref[b, at, :] = basis_in
            part = mm(basis_in, bases_ref[b])
            conv = part if conv is None else conv + part
        conv_ref[at, :] = conv
    row, lane = iota((8, LANES), 0), iota((8, LANES), 1)
    total = jnp.zeros((8, LANES), f32)
    for b in range(basis_count):
        for r in range(relations):
            part = jnp.sum(sums[b][:, r * slots : (r + 1) * slots], axis=1, keepdims=True)
            total = jnp.where((row == r) & (lane == b), part, total)
    coef_grad_ref[...] = total
    arrive(5 + tiles)
    cot = cot_ref[...].astype(bf16)
    for b in range(basis_count):
        whole = mm(basis_ref[b], cot, TN)
        store_halves(place_ref, whole, mine_ref, theirs_ref, slice(b * width, (b + 1) * width))


def add_kernel(a_ref, b_ref, out_ref):
    out_ref[...] = a_ref[...] + b_ref[...]


def choose(place_ref, first_bit, blocks, index):
    bit = first_bit
    while len(blocks) > 1:
        zero = bit_is_zero(place_ref, bit)
        pairs = [(blocks[i], blocks[i + 1]) for i in range(0, len(blocks), 2)]
        if index % 2:
            blocks = [jnp.where(zero, high, low) for low, high in pairs]
        else:
            blocks = [jnp.where(zero, low, high) for low, high in pairs]
        index //= 2
        bit += 1
    return blocks[0]


def scatter_kernel(place_ref, *refs, first_bit, beside, others):
    pieces, others = refs[:beside], refs[beside : beside + others]
    keep_ref, *send_refs = refs[beside + len(others) :]
    rows = keep_ref.shape[0]
    count = len(send_refs) + 1
    at = 0
    for piece in pieces:
        lanes = slice(at, at + piece.shape[1])
        blocks = []
        for i in range(count):
            rows_at = slice(i * rows, (i + 1) * rows)
            block = piece[rows_at, :].astype(f32)
            for other in others:
                block += other[rows_at, lanes].astype(f32)
            blocks.append(block)
        keep_ref[:, lanes] = choose(place_ref, first_bit, blocks, 0)
        for k in range(1, count):
            send_refs[k - 1][:, lanes] = choose(place_ref, first_bit, blocks, k).astype(send_refs[k - 1].dtype)
        at += piece.shape[1]


def total_kernel(*refs):
    out_ref = refs[-1]
    total = refs[0][...].astype(f32)
    for ref in refs[1:-1]:
        total += ref[...].astype(f32)
    out_ref[...] = total.astype(out_ref.dtype)


def join_kernel(place_ref, *refs, first_bit):
    out_ref = refs[-1]
    blocks = [ref[...] for ref in refs[:-1]]
    rows = blocks[0].shape[0]
    for i in range(len(blocks)):
        out_ref[i * rows : (i + 1) * rows, :] = choose(place_ref, first_bit, blocks, i)


def finish_kernel(
    place_ref, sum_mine_ref, sum_theirs_ref, mine_ref, theirs_ref, *refs, scale, value_at, outs
):
    holds, sems = refs[outs:-1], refs[-1]
    targets = []
    for out_ref in refs[:outs]:
        targets += [out_ref] if len(out_ref.shape) == 2 else [out_ref.at[b] for b in range(out_ref.shape[0])]
    zero = on_core_zero(place_ref)
    rows = mine_ref.shape[0]
    width = holds[0].shape[1]
    moves = []
    for i, hold in enumerate(holds):
        for p in range(width // LANES):
            at = slice(p * LANES, (p + 1) * LANES)
            source = slice(i * width + p * LANES, i * width + (p + 1) * LANES)
            if i == value_at:
                dkv, _ = load_summary(place_ref, p, width // LANES, sum_mine_ref, sum_theirs_ref)
                dkv = block_diagonal(dkv)
                a = mm_exact_left(mine_ref[:, source], dkv) * scale
                b = mm_exact_left(theirs_ref[:, source], dkv) * scale
            else:
                a = mine_ref[:, source].astype(f32) * scale
                b = theirs_ref[:, source].astype(f32) * scale
            hold[:rows, at] = jnp.where(zero, a, b)
            hold[rows:, at] = jnp.where(zero, b, a)
        moves.append(pltpu.make_async_copy(hold, targets[i], sems.at[i]))
        moves[-1].start()
    for move in moves:
        move.wait()


def swap_cores(x):
    return lax.ppermute(x, "outer", [(0, 1), (1, 0)])


def swap_nodes(x, bit):
    nodes = lax.axis_size("nodes")
    return lax.ppermute(x, "nodes", [(i, i ^ (1 << bit)) for i in range(nodes)])


def run_all(plan, step, x):
    return [y for y in [run(x) for run in plan.get(step, [])] if y is not None]


def sum_summary(mine, theirs, bits, beside):
    out = [shape(*mine.shape)]
    received = swap_cores(theirs)
    (mine,) = call(add_kernel, out, [mine, received], beside("core", mine))
    for bit in bits:
        received = swap_nodes(mine, bit)
        (mine,) = call(add_kernel, out, [mine, received], beside(bit, mine))
    return mine, swap_cores(mine), beside("back", mine)


def exchange(sends, first_bit):
    nodes = lax.axis_size("nodes")
    return [
        lax.ppermute(x, "nodes", [(i, i ^ (k << first_bit)) for i in range(nodes)])
        for k, x in enumerate(sends, start=1)
    ]


def per_device(
    features, w_query, w_key, w_value, bases, rel_coef, send_rows, tile_src, tile_dst, tile_count, cotangent
):
    rows, width = features.shape
    nodes = lax.axis_size("nodes")
    scale = 1.0 / math.sqrt(rows * nodes * lax.axis_size("outer"))
    basis_count = bases.shape[0]
    slots = send_rows.shape[2]
    halo_rows = nodes * slots
    table_rows = rows + halo_rows
    core, node = lax.axis_index("outer"), lax.axis_index("nodes")
    place = jnp.stack([core] + [(node >> bit) & 1 for bit in range(7)]).astype(jnp.int32)
    place = jnp.broadcast_to(place[:, None], (8, LANES))
    send, src, dst, count = send_rows[0], tile_src[0], tile_dst[0], tile_count[0]
    relations, tiles, cap = src.shape
    bits = list(range(nodes.bit_length() - 1))
    y, z1, z2 = bits[-3:]

    square, square_half = shape(rows, width), shape(rows, width, dtype=bf16)
    summary = shape(HEAD_DIM + 8, width // 2)
    wide_summary = shape(HEAD_DIM + 16, width // 2)

    def halves(n):
        return shape(width // 2, n * width), shape(width // 2, n * width, dtype=bf16)

    grads = shape(tiles, basis_count * TILE, width, dtype=bf16)
    kv_mine, kv_theirs, outgoing, grad_high, grad_low, exp_query, exp_key, values = call(
        start_kernel,
        [summary, summary, shape(halo_rows, width, dtype=bf16), grads, grads],
        [place],
        (),
        16,
        far=[features, w_query, w_key, w_value, send, bases, cotangent],
        us=5.5,
        lazy=True,
        far_outs=[square, square, square],
    )
    halo = lax.all_to_all(
        outgoing.reshape(nodes, slots, width), "nodes", split_axis=0, concat_axis=0, tiled=True
    ).reshape(halo_rows, width)

    kept = {}

    def run_backward(t, x):
        last = t == tiles - 1
        sent = [shape(halo_rows, width, dtype=bf16)] if last else []
        kept["table"], *sent, kept["mixed", t] = call(
            functools.partial(backward_kernel, tile=t, last=last),
            [shape(table_rows, width), *sent],
            [count, rel_coef, src, dst, grad_high] + ([kept["table"]] if t > 0 else []),
            [x],
            table_rows // 64,
            us=2.1,
            far_outs=[shape(2 * basis_count * TILE, table_rows, dtype=bf16)],
        )
        if last:
            kept["returned"] = lax.all_to_all(
                sent[0].reshape(nodes, slots, width), "nodes", split_axis=0, concat_axis=0, tiled=True
            ).reshape(halo_rows, width)
        return kept["table"]

    def run_forward(x):
        kept["conv"], kept["coef"], *kept["bases"] = call(
            forward_kernel,
            [square, shape(8, LANES), *halves(basis_count)],
            [count, rel_coef, place, src, dst],
            [x],
            8 + table_rows // 64,
            far=[features, halo, grad_high, grad_low, bases, *[kept["mixed", t] for t in range(tiles)], cotangent],
            us=9,
            lazy=True,
            scratch=[shape(basis_count, rows, width, dtype=bf16)],
        )
        return None

    backward = [functools.partial(run_backward, t) for t in range(tiles)]
    first = {bits[0]: backward[:1], y: backward[1:2], z1: backward[2:3], z2: backward[3:], "back": [run_forward]}
    kv_mine, kv_theirs, after = sum_summary(
        kv_mine, kv_theirs, bits, functools.partial(run_all, first)
    )
    dkv_mine, dkv_theirs, qblock, layer_out = call(
        attend_kernel,
        [wide_summary, wide_summary, square_half],
        [place, exp_query, cotangent, kv_mine, kv_theirs, kept["coef"], kept["conv"]],
        after,
        us=2.7,
        far_outs=[square],
    )

    plane, planes = nodes // 4, 4
    plane_rows = width // 2 // plane
    place_rows = plane_rows // planes
    early_count = basis_count + 2
    early_width = early_count * width

    def scatter(operands, first_bit, count, n_rows, beside=1, after=()):
        columns = sum(x.shape[1] for x in operands[:beside])
        own, *out = call(
            functools.partial(
                scatter_kernel, first_bit=first_bit, beside=beside, others=len(operands) - beside
            ),
            [shape(n_rows, columns)] + [shape(n_rows, columns, dtype=bf16 if n_rows >= 16 else f32)] * (count - 1),
            [place, *operands],
            after,
            12,
        )
        return [own, *exchange(out, first_bit)]

    def gather(own, first_bit, count, after=()):
        outs = [shape(own.shape[0] * count, own.shape[1], dtype=own.dtype)]
        blocks = [own, *exchange([own] * (count - 1), first_bit)]
        return call(functools.partial(join_kernel, first_bit=first_bit), outs, [place, *blocks], after)[0]

    def total(blocks, after=()):
        out = shape(*blocks[0].shape, dtype=bf16 if blocks[0].shape[0] >= 16 else f32)
        return call(total_kernel, [out], blocks, after)[0]

    def finish(own, bodies, value_at):
        count = sum(max(n, 1) for n in bodies)
        return pl.pallas_call(
            functools.partial(finish_kernel, scale=scale, value_at=value_at, outs=len(bodies)),
            out_shape=[shape(n, width, width) if n else shape(width, width) for n in bodies],
            in_specs=[VMEM] * 5,
            out_specs=[HBM] * len(bodies),
            scratch_shapes=[pltpu.VMEM((width, width), f32)] * count + [pltpu.SemaphoreType.DMA((count,))],
            compiler_params=pltpu.CompilerParams(vmem_limit_bytes=12 * 1024 * 1024),
            cost_estimate=pl.CostEstimate(flops=int(count * 0.8e9), bytes_accessed=0, transcendentals=0),
        )(place, dkv_mine, dkv_theirs, own, swap_cores(own))

    def run_returned(x):
        (kept["graph"],) = call(
            returned_kernel, [square], [send, kept["table"], kept["returned"]], [x], us=0.5
        )
        return kept["graph"]

    def run_query(x):
        kept["early"] = call(
            query_kernel,
            [halves(2)[0], halves(early_count)[1]],
            [place, qblock, exp_key, kept["bases"][1]],
            [x],
            12,
            far=[features],
            us=1.8,
        )
        return kept["early"][1]

    def run_early_plane(x):
        operands = [kept["bases"][0], kept["early"][0], swap_cores(kept["early"][1])]
        kept["blocks"] = scatter(operands, 0, plane, plane_rows, 2, [x])
        return kept["blocks"][0]

    def run_early_sum(x):
        (kept["early sum"],) = call(total_kernel, [shape(plane_rows, early_width)], kept["blocks"], [x])
        return kept["early sum"]

    second = {"core": [run_returned], bits[0]: [run_query], z1: [run_early_plane], "back": [run_early_sum]}
    dkv_mine, dkv_theirs, after = sum_summary(dkv_mine, dkv_theirs, bits, functools.partial(run_all, second))
    kblock, key_mine, key_theirs = call(
        key_kernel,
        [square_half, *halves(1)],
        [place, exp_key, values, dkv_mine, dkv_theirs],
        after,
        far=[features],
        us=1.8,
    )
    key = scatter([key_mine, swap_cores(key_theirs)], 0, plane, plane_rows)
    (key,) = call(total_kernel, [shape(plane_rows, width)], key)
    own = scatter([kept["early sum"], key], z1, planes, place_rows, 2)
    own = total(own)
    cut = (basis_count + 1) * width
    own, last = own[:, :cut], own[:, cut:]
    own = gather(own, z1, planes).astype(bf16)
    grad_x, token = call(
        input_grad_kernel,
        [square, shape(8, LANES)],
        [place, qblock, kblock, exp_key, dkv_mine, dkv_theirs, kept["graph"]],
        [own],
        16,
        far=[w_query, w_key, w_value],
        us=3.5,
    )
    last = gather(last, z1, planes, [token]).astype(bf16)
    own = gather(own, 0, plane)
    last = gather(last, 0, plane)
    bases_grad, query_grad = finish(own, [basis_count, 0], -1)
    value_grad, key_grad = finish(last, [0, 0], 0)
    coef_sum = jnp.where(core == 0, dkv_mine, dkv_theirs)[HEAD_DIM + 8 :, :]
    coef_grad = coef_sum[:relations, :basis_count] * scale
    return layer_out, grad_x, query_grad, key_grad, value_grad, bases_grad, coef_grad


def solution(mesh):
    both = ("outer", "nodes")
    in_specs = (
        P(both, None),
        P(),
        P(),
        P(),
        P(),
        P(),
        P(both, None, None),
        P(both, None, None, None),
        P(both, None, None, None),
        P(both, None, None),
        P(both, None),
    )
    out_specs = (P(both, None), P(both, None), P(), P(), P(), P(), P())
    return jax.shard_map(per_device, mesh=mesh, in_specs=in_specs, out_specs=out_specs, check_vma=False)
```

```python
import functools
import math

import jax
import jax.numpy as jnp
from jax import lax
from jax.experimental import pallas as pl
from jax.experimental.pallas import tpu as pltpu
from jax.sharding import PartitionSpec as P

HEAD_DIM = 64
TILE = 128
LANES = 128

f32 = jnp.float32
bf16 = jnp.bfloat16
NN = (((1,), (0,)), ((), ()))
NT = (((1,), (1,)), ((), ()))
TN = (((0,), (0,)), ((), ()))

VMEM = pl.BlockSpec(memory_space=pltpu.VMEM)
HBM = pl.BlockSpec(memory_space=pltpu.HBM)


def shape(*dims, dtype=f32):
    return jax.ShapeDtypeStruct(dims, dtype)


def call(body, outs, arrays, after=(), megabytes=8, far=(), us=0.3, lazy=False, scratch=(), far_outs=()):
    n_in, n_after, n_far = len(arrays), len(after), len(far)
    n_outs, n_leave = len(outs), len(far_outs)

    def kernel(*refs):
        refs = list(refs)

        def take(n):
            taken = refs[:n]
            del refs[:n]
            return taken

        given, _, sources, results, leaving = take(n_in), take(n_after), take(n_far), take(n_outs), take(n_leave)
        targets, held, more = take(n_far), take(n_leave), take(len(scratch))
        moves = [pltpu.make_async_copy(sources[i], targets[i], refs[0].at[i]) for i in range(n_far)]
        leaves = [pltpu.make_async_copy(held[i], leaving[i], refs[0].at[n_far + i]) for i in range(n_leave)]
        for move in moves:
            move.start()
        options = {}
        if lazy:
            options["arrive"] = lambda i: moves[i].wait()
        else:
            for move in moves:
                move.wait()
        if far_outs:
            options["leave"] = lambda i: leaves[i].start()
        body(*given, *targets, *results, *held, *more, **options)
        for leave in leaves:
            leave.wait()

    scratches = [pltpu.VMEM(x.shape, x.dtype) for x in (*far, *far_outs, *scratch)]
    sems = n_far + n_leave
    return pl.pallas_call(
        kernel,
        out_shape=list(outs) + [pltpu.HBM(x.shape, x.dtype) for x in far_outs],
        in_specs=[VMEM] * (n_in + n_after) + [HBM] * n_far,
        out_specs=[VMEM] * n_outs + [HBM] * n_leave,
        scratch_shapes=scratches + ([pltpu.SemaphoreType.DMA((sems,))] if sems else []),
        compiler_params=pltpu.CompilerParams(vmem_limit_bytes=megabytes * 1024 * 1024),
        cost_estimate=pl.CostEstimate(
            flops=int(us * 1.1e9),
            bytes_accessed=sum(x.size * x.dtype.itemsize for x in arrays),
            transcendentals=0,
        ),
    )(*arrays, *after, *[pltpu.with_memory_space_constraint(x, pltpu.HBM) for x in far])


def on_core_zero(place_ref):
    return place_ref[0:1, 0:1] == 0


def bit_is_zero(place_ref, bit):
    return place_ref[1 + bit : 2 + bit, 0:1] == 0


def mm(a, b, dims=NN):
    return lax.dot_general(a, b, dims, preferred_element_type=f32)


def split(x):
    high = x.astype(bf16)
    return high, (x - high.astype(f32)).astype(bf16)


def mm_exact_right(a, b, dims=NN):
    high, low = split(a)
    return mm(high, b, dims) + mm(low, b, dims)


def mm_exact_left(a, b, dims=NN):
    high, low = split(b)
    return mm(a, high, dims) + mm(a, low, dims)


def mm_wide(a, b, dims=NN):
    ah, al = split(a)
    bh, bl = split(b)
    return mm(ah, bh, dims) + (mm(ah, bl, dims) + mm(al, bh, dims))


def iota(dims, axis):
    return lax.broadcasted_iota(jnp.int32, dims, axis)


def one_hot_rows(index_row, count):
    return jnp.where(iota((count, index_row.shape[1]), 0) == index_row, 1.0, 0.0).astype(bf16)


def head_mask():
    return (iota((LANES, LANES), 0) < HEAD_DIM) == (iota((LANES, LANES), 1) < HEAD_DIM)


def block_diagonal(packed):
    return jnp.where(head_mask(), jnp.concatenate([packed, packed], axis=0), 0.0)


def pack_diagonal(full):
    left = iota((HEAD_DIM, LANES), 1) < HEAD_DIM
    return jnp.where(left, full[:HEAD_DIM], full[HEAD_DIM:])


def store_summary(place_ref, packed, rows, mine_ref, theirs_ref, extra=None):
    zero = on_core_zero(place_ref)
    half = len(packed) // 2
    first = iota((8, LANES), 0) == 0
    if extra is not None:
        at = slice(HEAD_DIM + 8, HEAD_DIM + 16)
        mine_ref[at, :] = jnp.zeros((8, mine_ref.shape[1]), f32)
        theirs_ref[at, :] = jnp.zeros((8, mine_ref.shape[1]), f32)
        mine_ref[at, :LANES] = jnp.where(zero, extra, 0.0)
        theirs_ref[at, :LANES] = jnp.where(zero, 0.0, extra)
    for p in range(half):
        at = slice(p * LANES, (p + 1) * LANES)
        low = jnp.concatenate([packed[p], jnp.where(first, rows[p], 0.0)], axis=0)
        high = jnp.concatenate([packed[p + half], jnp.where(first, rows[p + half], 0.0)], axis=0)
        mine_ref[: HEAD_DIM + 8, at] = jnp.where(zero, low, high)
        theirs_ref[: HEAD_DIM + 8, at] = jnp.where(zero, high, low)


def load_summary(place_ref, pair, pairs, mine_ref, theirs_ref):
    half = pairs // 2
    at = slice(pair % half * LANES, (pair % half + 1) * LANES)
    low, high = (mine_ref, theirs_ref) if pair < half else (theirs_ref, mine_ref)
    both = jnp.where(on_core_zero(place_ref), low[:, at], high[:, at])
    return both[:HEAD_DIM], both[HEAD_DIM : HEAD_DIM + 1]


def store_halves(place_ref, whole, mine_ref, theirs_ref, at):
    zero = on_core_zero(place_ref)
    rows = whole.shape[0] // 2
    low, high = whole[:rows], whole[rows:]
    mine_ref[:, at] = jnp.where(zero, low, high)
    theirs_ref[:, at] = jnp.where(zero, high, low).astype(bf16)


def send_row(send_ref):
    return jnp.concatenate([send_ref[p : p + 1, :] for p in range(send_ref.shape[0])], axis=1)


def start_kernel(
    place_ref,
    features_ref,
    wq_ref,
    wk_ref,
    wv_ref,
    send_ref,
    bases_ref,
    cot_ref,
    mine_ref,
    theirs_ref,
    out_ref,
    high_ref,
    low_ref,
    eq_ref,
    ek_ref,
    v_ref,
    *,
    arrive,
    leave,
):
    pairs = features_ref.shape[1] // LANES
    arrive(0)
    features = features_ref[...]
    arrive(1)
    eq_ref[...] = jnp.exp(mm(features, wq_ref[...]))
    leave(0)
    arrive(2)
    ek_ref[...] = jnp.exp(mm(features, wk_ref[...]))
    leave(1)
    arrive(3)
    v_ref[...] = mm(features, wv_ref[...])
    leave(2)
    packed, sums = [], []
    for p in range(pairs):
        at = slice(p * LANES, (p + 1) * LANES)
        key = ek_ref[:, at]
        packed.append(pack_diagonal(mm_wide(key, v_ref[:, at], TN)))
        sums.append(jnp.sum(key, axis=0, keepdims=True))
    store_summary(place_ref, packed, sums, mine_ref, theirs_ref)
    arrive(4)
    pick = one_hot_rows(send_row(send_ref), features.shape[0])
    out_ref[...] = mm(pick, features, TN).astype(bf16)
    arrive(5)
    arrive(6)
    cot = cot_ref[...].astype(bf16)
    for b in range(bases_ref.shape[0]):
        high, low = split(mm(cot, bases_ref[b], NT))
        for t in range(high_ref.shape[0]):
            high_ref[t, b * TILE : (b + 1) * TILE, :] = high[t * TILE : (t + 1) * TILE]
            low_ref[t, b * TILE : (b + 1) * TILE, :] = low[t * TILE : (t + 1) * TILE]


def attend_kernel(
    place_ref,
    eq_ref,
    cot_ref,
    sum_mine_ref,
    sum_theirs_ref,
    coef_ref,
    conv_ref,
    mine_ref,
    theirs_ref,
    qblock_ref,
    layer_ref,
    *,
    leave,
):
    pairs = eq_ref.shape[1] // LANES
    same_head = jnp.where(head_mask(), 1.0, 0.0).astype(bf16)
    packed, sums = [], []
    for p in range(pairs):
        at = slice(p * LANES, (p + 1) * LANES)
        kv, ks = load_summary(place_ref, p, pairs, sum_mine_ref, sum_theirs_ref)
        kv = block_diagonal(kv)
        query = eq_ref[:, at]
        cot = cot_ref[:, at]
        inverse = 1.0 / mm_exact_right(query * ks, same_head)
        attended = mm_wide(query, kv) * inverse
        layer_ref[:, at] = attended + conv_ref[:, at]
        num_grad = cot * inverse
        den_grad = -mm_exact_right(cot * attended, same_head) * inverse
        packed.append(pack_diagonal(mm_wide(query, num_grad, TN)))
        sums.append(jnp.sum(query * den_grad, axis=0, keepdims=True))
        query_side = mm_wide(num_grad, kv, NT) + den_grad * ks
        qblock_ref[:, at] = (query_side * query).astype(bf16)
    leave(0)
    store_summary(place_ref, packed, sums, mine_ref, theirs_ref, coef_ref[...])


def query_kernel(place_ref, qblock_ref, ek_ref, bases_theirs_ref, features_ref, mine_ref, theirs_ref):
    width = features_ref.shape[1]
    bases_width = bases_theirs_ref.shape[1]
    theirs_ref[:, :bases_width] = bases_theirs_ref[...]
    theirs_ref = theirs_ref.at[:, bases_width:]
    features = features_ref[...]
    store_halves(place_ref, mm(features, qblock_ref[...], TN), mine_ref, theirs_ref, slice(0, width))
    whole = mm_exact_left(features, ek_ref[...], TN)
    store_halves(place_ref, whole, mine_ref, theirs_ref, slice(width, 2 * width))


def key_kernel(
    place_ref, ek_ref, v_ref, sum_mine_ref, sum_theirs_ref, features_ref, kblock_ref, mine_ref, theirs_ref, *, arrive
):
    pairs = ek_ref.shape[1] // LANES
    for p in range(pairs):
        at = slice(p * LANES, (p + 1) * LANES)
        dkv, dks = load_summary(place_ref, p, pairs, sum_mine_ref, sum_theirs_ref)
        key_side = mm_wide(v_ref[:, at], block_diagonal(dkv), NT) + dks
        kblock_ref[:, at] = (key_side * ek_ref[:, at]).astype(bf16)
    arrive(0)
    store_halves(place_ref, mm(features_ref[...], kblock_ref[...], TN), mine_ref, theirs_ref, slice(None))


def returned_kernel(send_ref, table_ref, returned_ref, out_ref):
    rows = out_ref.shape[0]
    out_ref[...] = table_ref[:rows, :] + mm(one_hot_rows(send_row(send_ref), rows), returned_ref[...])


def input_grad_kernel(
    place_ref,
    qblock_ref,
    kblock_ref,
    ek_ref,
    sum_mine_ref,
    sum_theirs_ref,
    graph_ref,
    wq_ref,
    wk_ref,
    wv_ref,
    out_ref,
    token_ref,
):
    token_ref[...] = jnp.zeros((8, LANES), f32)
    pairs = ek_ref.shape[1] // LANES
    blocks = []
    for p in range(pairs):
        at = slice(p * LANES, (p + 1) * LANES)
        dkv, _ = load_summary(place_ref, p, pairs, sum_mine_ref, sum_theirs_ref)
        blocks.append(mm_wide(ek_ref[:, at], block_diagonal(dkv)).astype(bf16))
    total = mm(qblock_ref[...], wq_ref[...], NT) + mm(kblock_ref[...], wk_ref[...], NT)
    out_ref[...] = total + mm(jnp.concatenate(blocks, axis=1), wv_ref[...], NT) + graph_ref[...]


def tile_incidence(count_ref, dst_ref, tile):
    relations, _, slots = dst_ref.shape
    hits = []
    for r in range(relations):
        live = iota((TILE, slots), 1) < count_ref[r : r + 1, tile : tile + 1]
        target = iota((TILE, slots), 0) == dst_ref[r, tile : tile + 1, :]
        hits.append(jnp.where(target & live, 1.0, 0.0))
    ours = jnp.where(iota((relations * slots, LANES), 0) // slots == iota((relations * slots, LANES), 1), 1.0, 0.0)
    degree = mm(jnp.concatenate(hits, axis=1).astype(bf16), ours.astype(bf16))
    inverse = 1.0 / jnp.maximum(degree, 1.0)
    return [hit * inverse[:, r : r + 1] for r, hit in enumerate(hits)]


def tile_pick(src_ref, tile, table_rows):
    picks = [one_hot_rows(src_ref[r, tile : tile + 1, :], table_rows) for r in range(src_ref.shape[0])]
    return jnp.concatenate(picks, axis=1)


def backward_kernel(count_ref, coef_ref, src_ref, dst_ref, grad_ref, *refs, tile, last, leave):
    mixed_ref = refs[-1]
    table_ref = refs[0 if tile == 0 else 1]
    hits = tile_incidence(count_ref, dst_ref, tile)
    scaled = [
        jnp.concatenate([hit * coef_ref[r : r + 1, b : b + 1] for r, hit in enumerate(hits)], axis=1)
        for b in range(coef_ref.shape[1])
    ]
    high, low = split(jnp.concatenate(scaled, axis=0))
    both = mm(jnp.concatenate([high, low], axis=0), tile_pick(src_ref, tile, table_ref.shape[0]), NT)
    wide = both.shape[0] // 2
    high, low = split(both[:wide] + both[wide:])
    mixed_ref[:wide, :] = high
    mixed_ref[wide:, :] = low
    leave(0)
    table = mm(high, grad_ref[tile], TN)
    table = table if tile == 0 else table + refs[0][...]
    table_ref[...] = table
    if last:
        sent_ref = refs[-2]
        sent_ref[...] = table[table.shape[0] - sent_ref.shape[0] :, :].astype(bf16)


def forward_kernel(count_ref, place_ref, src_ref, dst_ref, *refs, arrive):
    relations, tiles, slots = src_ref.shape
    own_ref, halo_ref, high_ref, low_ref, bases_ref = refs[:5]
    mixed_refs, refs = refs[5 : 5 + tiles], refs[5 + tiles :]
    cot_ref, conv_ref, coef_grad_ref, mine_ref, theirs_ref, basis_ref, table_ref = refs
    basis_count = bases_ref.shape[0]
    wide = basis_count * TILE
    rows, width = own_ref.shape
    sums = [jnp.zeros((1, relations * slots), f32) for _ in range(basis_count)]
    for t in range(tiles):
        hit = jnp.concatenate(tile_incidence(count_ref, dst_ref, t), axis=1)
        pick = tile_pick(src_ref, t, table_ref.shape[0])
        if t == 0:
            for i in range(4):
                arrive(i)
            table_ref[:rows, :] = own_ref[...]
            table_ref[rows:, :] = halo_ref[...]
        dots = mm(jnp.concatenate([high_ref[t], low_ref[t]], axis=0), table_ref[...], NT)
        edge = mm((dots[:wide] + dots[wide:]).astype(bf16), pick)
        for b in range(basis_count):
            sums[b] += jnp.sum(edge[b * TILE : (b + 1) * TILE] * hit, axis=0, keepdims=True)
        if t == 0:
            arrive(4)
        arrive(5 + t)
        both = mm(mixed_refs[t][...], table_ref[...])
        both = (both[:wide] + both[wide:]).astype(bf16)
        at = slice(t * TILE, (t + 1) * TILE)
        conv = None
        for b in range(basis_count):
            basis_in = both[b * TILE : (b + 1) * TILE]
            basis_ref[b, at, :] = basis_in
            part = mm(basis_in, bases_ref[b])
            conv = part if conv is None else conv + part
        conv_ref[at, :] = conv
    row, lane = iota((8, LANES), 0), iota((8, LANES), 1)
    total = jnp.zeros((8, LANES), f32)
    for b in range(basis_count):
        for r in range(relations):
            part = jnp.sum(sums[b][:, r * slots : (r + 1) * slots], axis=1, keepdims=True)
            total = jnp.where((row == r) & (lane == b), part, total)
    coef_grad_ref[...] = total
    arrive(5 + tiles)
    cot = cot_ref[...].astype(bf16)
    for b in range(basis_count):
        whole = mm(basis_ref[b], cot, TN)
        store_halves(place_ref, whole, mine_ref, theirs_ref, slice(b * width, (b + 1) * width))


def copy_kernel(a_ref, out_ref):
    out_ref[...] = a_ref[...]


def add_kernel(a_ref, b_ref, out_ref):
    out_ref[...] = a_ref[...] + b_ref[...]


def choose(place_ref, first_bit, blocks, index):
    bit = first_bit
    while len(blocks) > 1:
        zero = bit_is_zero(place_ref, bit)
        pairs = [(blocks[i], blocks[i + 1]) for i in range(0, len(blocks), 2)]
        if index % 2:
            blocks = [jnp.where(zero, high, low) for low, high in pairs]
        else:
            blocks = [jnp.where(zero, low, high) for low, high in pairs]
        index //= 2
        bit += 1
    return blocks[0]


def scatter_kernel(place_ref, *refs, first_bit, beside, others):
    pieces, others = refs[:beside], refs[beside : beside + others]
    keep_ref, *send_refs = refs[beside + len(others) :]
    rows = keep_ref.shape[0]
    count = len(send_refs) + 1
    at = 0
    for piece in pieces:
        lanes = slice(at, at + piece.shape[1])
        blocks = []
        for i in range(count):
            rows_at = slice(i * rows, (i + 1) * rows)
            block = piece[rows_at, :].astype(f32)
            for other in others:
                block += other[rows_at, lanes].astype(f32)
            blocks.append(block)
        keep_ref[:, lanes] = choose(place_ref, first_bit, blocks, 0)
        for k in range(1, count):
            send_refs[k - 1][:, lanes] = choose(place_ref, first_bit, blocks, k).astype(send_refs[k - 1].dtype)
        at += piece.shape[1]


def total_kernel(*refs):
    out_ref = refs[-1]
    total = refs[0][...].astype(f32)
    for ref in refs[1:-1]:
        total += ref[...].astype(f32)
    out_ref[...] = total.astype(out_ref.dtype)


def join_kernel(place_ref, *refs, first_bit):
    out_ref = refs[-1]
    blocks = [ref[...] for ref in refs[:-1]]
    rows = blocks[0].shape[0]
    for i in range(len(blocks)):
        out_ref[i * rows : (i + 1) * rows, :] = choose(place_ref, first_bit, blocks, i).astype(out_ref.dtype)


def finish_kernel(
    place_ref, sum_mine_ref, sum_theirs_ref, mine_ref, theirs_ref, *refs, scale, value_at, outs, after
):
    refs = refs[after:]
    refs[outs][...] = jnp.zeros((8, LANES), f32)
    holds, sems = refs[outs + 1 : -1], refs[-1]
    targets = []
    for out_ref in refs[:outs]:
        targets += [out_ref] if len(out_ref.shape) == 2 else [out_ref.at[b] for b in range(out_ref.shape[0])]
    zero = on_core_zero(place_ref)
    rows = mine_ref.shape[0]
    width = holds[0].shape[1]
    moves = []
    for i, hold in enumerate(holds):
        for p in range(width // LANES):
            at = slice(p * LANES, (p + 1) * LANES)
            source = slice(i * width + p * LANES, i * width + (p + 1) * LANES)
            if i == value_at:
                dkv, _ = load_summary(place_ref, p, width // LANES, sum_mine_ref, sum_theirs_ref)
                dkv = block_diagonal(dkv)
                a = mm_exact_left(mine_ref[:, source], dkv) * scale
                b = mm_exact_left(theirs_ref[:, source], dkv) * scale
            else:
                a = mine_ref[:, source].astype(f32) * scale
                b = theirs_ref[:, source].astype(f32) * scale
            hold[:rows, at] = jnp.where(zero, a, b)
            hold[rows:, at] = jnp.where(zero, b, a)
        moves.append(pltpu.make_async_copy(hold, targets[i], sems.at[i]))
        moves[-1].start()
    for move in moves:
        move.wait()


def swap_cores(x):
    return lax.ppermute(x, "outer", [(0, 1), (1, 0)])


def swap_nodes(x, bit):
    nodes = lax.axis_size("nodes")
    return lax.ppermute(x, "nodes", [(i, i ^ (1 << bit)) for i in range(nodes)])


def run_all(plan, step, x):
    return [y for y in [run(x) for run in plan.get(step, [])] if y is not None]


def sum_summary(mine, theirs, bits, beside):
    out = [shape(*mine.shape)]
    received = swap_cores(theirs)
    (mine,) = call(add_kernel, out, [mine, received], beside("core", mine))
    for bit in bits:
        received = swap_nodes(mine, bit)
        (mine,) = call(add_kernel, out, [mine, received], beside(bit, mine))
    return mine, swap_cores(mine), beside("back", mine)


def exchange(sends, first_bit):
    nodes = lax.axis_size("nodes")
    return [
        lax.ppermute(x, "nodes", [(i, i ^ (k << first_bit)) for i in range(nodes)])
        for k, x in enumerate(sends, start=1)
    ]


def per_device(
    features, w_query, w_key, w_value, bases, rel_coef, send_rows, tile_src, tile_dst, tile_count, cotangent
):
    rows, width = features.shape
    nodes = lax.axis_size("nodes")
    scale = 1.0 / math.sqrt(rows * nodes * lax.axis_size("outer"))
    basis_count = bases.shape[0]
    slots = send_rows.shape[2]
    halo_rows = nodes * slots
    table_rows = rows + halo_rows
    core, node = lax.axis_index("outer"), lax.axis_index("nodes")
    place = jnp.stack([core] + [(node >> bit) & 1 for bit in range(7)]).astype(jnp.int32)
    place = jnp.broadcast_to(place[:, None], (8, LANES))
    send, src, dst, count = send_rows[0], tile_src[0], tile_dst[0], tile_count[0]
    relations, tiles, cap = src.shape
    bits = list(range(nodes.bit_length() - 1))
    y, z1, z2 = bits[-3:]

    square, square_half = shape(rows, width), shape(rows, width, dtype=bf16)
    summary = shape(HEAD_DIM + 8, width // 2)
    wide_summary = shape(HEAD_DIM + 16, width // 2)

    def halves(n):
        return shape(width // 2, n * width), shape(width // 2, n * width, dtype=bf16)

    grads = shape(tiles, basis_count * TILE, width, dtype=bf16)
    kv_mine, kv_theirs, outgoing, grad_high, grad_low, exp_query, exp_key, values = call(
        start_kernel,
        [summary, summary, shape(halo_rows, width, dtype=bf16), grads, grads],
        [place],
        (),
        16,
        far=[features, w_query, w_key, w_value, send, bases, cotangent],
        us=5.5,
        lazy=True,
        far_outs=[square, square, square],
    )
    halo = lax.all_to_all(
        outgoing.reshape(nodes, slots, width), "nodes", split_axis=0, concat_axis=0, tiled=True
    ).reshape(halo_rows, width)

    kept = {}

    def run_backward(t, x):
        last = t == tiles - 1
        sent = [shape(halo_rows, width, dtype=bf16)] if last else []
        kept["table"], *sent, kept["mixed", t] = call(
            functools.partial(backward_kernel, tile=t, last=last),
            [shape(table_rows, width), *sent],
            [count, rel_coef, src, dst, grad_high] + ([kept["table"]] if t > 0 else []),
            [x],
            table_rows // 64,
            us=2.1,
            far_outs=[shape(2 * basis_count * TILE, table_rows, dtype=bf16)],
        )
        if last:
            kept["returned"] = lax.all_to_all(
                sent[0].reshape(nodes, slots, width), "nodes", split_axis=0, concat_axis=0, tiled=True
            ).reshape(halo_rows, width)
        return kept["table"]

    def run_forward(x):
        kept["conv"], kept["coef"], *kept["bases"] = call(
            forward_kernel,
            [square, shape(8, LANES), *halves(basis_count)],
            [count, place, src, dst],
            [x],
            8 + table_rows // 64,
            far=[features, halo, grad_high, grad_low, bases, *[kept["mixed", t] for t in range(tiles)], cotangent],
            us=9,
            lazy=True,
            scratch=[shape(basis_count, rows, width, dtype=bf16), shape(table_rows, width, dtype=bf16)],
        )
        return None

    backward = [functools.partial(run_backward, t) for t in range(tiles)]
    first = {bits[0]: backward[:1], y: backward[1:2], z1: backward[2:3], z2: backward[3:], "back": [run_forward]}
    kv_mine, kv_theirs, after = sum_summary(
        kv_mine, kv_theirs, bits, functools.partial(run_all, first)
    )
    dkv_mine, dkv_theirs, qblock, layer_out = call(
        attend_kernel,
        [wide_summary, wide_summary, square_half],
        [place, exp_query, cotangent, kv_mine, kv_theirs, kept["coef"], kept["conv"]],
        after,
        us=2.7,
        far_outs=[square],
    )

    plane, planes = nodes // 4, 4
    plane_rows = width // 2 // plane
    place_rows = plane_rows // planes
    early_count = basis_count + 2
    early_width = early_count * width

    def scatter(operands, first_bit, count, n_rows, beside=1, after=()):
        columns = sum(x.shape[1] for x in operands[:beside])
        own, *out = call(
            functools.partial(
                scatter_kernel, first_bit=first_bit, beside=beside, others=len(operands) - beside
            ),
            [shape(n_rows, columns)] + [shape(n_rows, columns, dtype=bf16 if n_rows >= 16 else f32)] * (count - 1),
            [place, *operands],
            after,
            12,
        )
        return [own, *exchange(out, first_bit)]

    def join(blocks, first_bit, after=()):
        own = blocks[0]
        rows = len(blocks) * own.shape[0]
        outs = [shape(rows, own.shape[1], dtype=bf16 if rows >= 16 else f32)]
        return call(functools.partial(join_kernel, first_bit=first_bit), outs, [place, *blocks], after)[0]

    def total(blocks, after=()):
        out = shape(*blocks[0].shape, dtype=bf16 if blocks[0].shape[0] >= 16 else f32)
        return call(total_kernel, [out], blocks, after)[0]

    def finish(own, bodies, value_at, after=()):
        count = sum(max(n, 1) for n in bodies)
        return pl.pallas_call(
            functools.partial(finish_kernel, scale=scale, value_at=value_at, outs=len(bodies), after=len(after)),
            out_shape=[shape(n, width, width) if n else shape(width, width) for n in bodies] + [shape(8, LANES)],
            in_specs=[VMEM] * (5 + len(after)),
            out_specs=[HBM] * len(bodies) + [VMEM],
            scratch_shapes=[pltpu.VMEM((width, width), f32)] * count + [pltpu.SemaphoreType.DMA((count,))],
            compiler_params=pltpu.CompilerParams(vmem_limit_bytes=12 * 1024 * 1024),
            cost_estimate=pl.CostEstimate(flops=int(count * 0.8e9), bytes_accessed=0, transcendentals=0),
        )(place, dkv_mine, dkv_theirs, own, swap_cores(own), *after)

    def run_returned(x):
        (kept["graph"],) = call(
            returned_kernel, [square], [send, kept["table"], kept["returned"]], [x], us=0.5
        )
        return kept["graph"]

    def run_query(x):
        kept["early"] = call(
            query_kernel,
            [halves(2)[0], halves(early_count)[1]],
            [place, qblock, exp_key, kept["bases"][1]],
            [x],
            12,
            far=[features],
            us=1.8,
        )
        return kept["early"][1]

    def run_early_plane(x):
        operands = [kept["bases"][0], kept["early"][0], swap_cores(kept["early theirs"])]
        kept["blocks"] = scatter(operands, 0, plane, plane_rows, 2, [x])
        return kept["blocks"][0]

    def run_early_line(x):
        kept["blocks"] = scatter(kept["blocks"], z1, planes, place_rows, 1, [x])
        return kept["blocks"][0]

    def run_early_theirs(x):
        (kept["early theirs"],) = call(copy_kernel, [halves(early_count)[1]], [kept["early"][1]], [x])
        return kept["early theirs"]

    second = {"core": [run_returned], bits[0]: [run_query], y: [run_early_theirs], z1: [run_early_plane]}
    second["back"] = [run_early_line]
    dkv_mine, dkv_theirs, after = sum_summary(dkv_mine, dkv_theirs, bits, functools.partial(run_all, second))
    kblock, key_mine, key_theirs = call(
        key_kernel,
        [square_half, *halves(1)],
        [place, exp_key, values, dkv_mine, dkv_theirs],
        after,
        far=[features],
        us=1.3,
        lazy=True,
    )
    def spread(x, first_bit, count):
        return [x, *exchange([x] * (count - 1), first_bit)]

    key = scatter([key_mine, swap_cores(key_theirs)], 0, plane, plane_rows)
    early = spread(total(kept["blocks"], [key[0]]), z1, planes)
    key = spread(total(key, [early[0]]), z1, planes)
    early = join(early, z1, [key[0]])
    key = spread(total(key), 0, plane)
    early = spread(early, 0, plane)
    key = join(key, 0, [early[0]])
    grad_x, token = call(
        input_grad_kernel,
        [square, shape(8, LANES)],
        [place, qblock, kblock, exp_key, dkv_mine, dkv_theirs, kept["graph"]],
        [key],
        16,
        far=[w_query, w_key, w_value],
        us=3.5,
    )
    key_grad, done = finish(key, [0], -1)
    early = join(early, 0, [token, done])
    bases_grad, query_grad, value_grad, _ = finish(early, [basis_count, 0, 0], basis_count + 1)
    coef_sum = jnp.where(core == 0, dkv_mine, dkv_theirs)[HEAD_DIM + 8 :, :]
    coef_grad = coef_sum[:relations, :basis_count] * scale
    return layer_out, grad_x, query_grad, key_grad, value_grad, bases_grad, coef_grad


def solution(mesh):
    both = ("outer", "nodes")
    in_specs = (
        P(both, None),
        P(),
        P(),
        P(),
        P(),
        P(),
        P(both, None, None),
        P(both, None, None, None),
        P(both, None, None, None),
        P(both, None, None),
        P(both, None),
    )
    out_specs = (P(both, None), P(both, None), P(), P(), P(), P(), P())
    return jax.shard_map(per_device, mesh=mesh, in_specs=in_specs, out_specs=out_specs, check_vma=False)
```

```python
import functools
import math

import jax
import jax.numpy as jnp
from jax import lax
from jax.experimental import pallas as pl
from jax.experimental.pallas import tpu as pltpu
from jax.sharding import PartitionSpec as P

HEAD_DIM = 64
TILE = 128
LANES = 128

f32 = jnp.float32
bf16 = jnp.bfloat16
NN = (((1,), (0,)), ((), ()))
NT = (((1,), (1,)), ((), ()))
TN = (((0,), (0,)), ((), ()))

VMEM = pl.BlockSpec(memory_space=pltpu.VMEM)
HBM = pl.BlockSpec(memory_space=pltpu.HBM)


def shape(*dims, dtype=f32):
    return jax.ShapeDtypeStruct(dims, dtype)


def call(body, outs, arrays, after=(), megabytes=8, far=(), us=0.3, lazy=False, scratch=(), far_outs=()):
    n_in, n_after, n_far = len(arrays), len(after), len(far)
    n_outs, n_leave = len(outs), len(far_outs)

    def kernel(*refs):
        refs = list(refs)

        def take(n):
            taken = refs[:n]
            del refs[:n]
            return taken

        given, _, sources, results, leaving = take(n_in), take(n_after), take(n_far), take(n_outs), take(n_leave)
        targets, held, more = take(n_far), take(n_leave), take(len(scratch))
        moves = [pltpu.make_async_copy(sources[i], targets[i], refs[0].at[i]) for i in range(n_far)]
        leaves = [pltpu.make_async_copy(held[i], leaving[i], refs[0].at[n_far + i]) for i in range(n_leave)]
        for move in moves:
            move.start()
        options = {}
        if lazy:
            options["arrive"] = lambda i: moves[i].wait()
        else:
            for move in moves:
                move.wait()
        if far_outs:
            options["leave"] = lambda i: leaves[i].start()
        body(*given, *targets, *results, *held, *more, **options)
        for leave in leaves:
            leave.wait()

    scratches = [pltpu.VMEM(x.shape, x.dtype) for x in (*far, *far_outs, *scratch)]
    sems = n_far + n_leave
    return pl.pallas_call(
        kernel,
        out_shape=list(outs) + [pltpu.HBM(x.shape, x.dtype) for x in far_outs],
        in_specs=[VMEM] * (n_in + n_after) + [HBM] * n_far,
        out_specs=[VMEM] * n_outs + [HBM] * n_leave,
        scratch_shapes=scratches + ([pltpu.SemaphoreType.DMA((sems,))] if sems else []),
        compiler_params=pltpu.CompilerParams(vmem_limit_bytes=megabytes * 1024 * 1024),
        cost_estimate=pl.CostEstimate(
            flops=int(us * 1.5e9),
            bytes_accessed=sum(x.size * x.dtype.itemsize for x in arrays),
            transcendentals=0,
        ),
    )(*arrays, *after, *[pltpu.with_memory_space_constraint(x, pltpu.HBM) for x in far])


def on_core_zero(place_ref):
    return place_ref[0:1, 0:1] == 0


def bit_is_zero(place_ref, bit):
    return place_ref[1 + bit : 2 + bit, 0:1] == 0


def mm(a, b, dims=NN):
    return lax.dot_general(a, b, dims, preferred_element_type=f32)


def split(x):
    high = x.astype(bf16)
    return high, (x - high.astype(f32)).astype(bf16)


def mm_exact_right(a, b, dims=NN):
    high, low = split(a)
    return mm(high, b, dims) + mm(low, b, dims)


def mm_exact_left(a, b, dims=NN):
    high, low = split(b)
    return mm(a, high, dims) + mm(a, low, dims)


def mm_wide(a, b, dims=NN):
    ah, al = split(a)
    bh, bl = split(b)
    return mm(ah, bh, dims) + (mm(ah, bl, dims) + mm(al, bh, dims))


def iota(dims, axis):
    return lax.broadcasted_iota(jnp.int32, dims, axis)


def one_hot_rows(index_row, count):
    return jnp.where(iota((count, index_row.shape[1]), 0) == index_row, 1.0, 0.0).astype(bf16)


def head_mask():
    return (iota((LANES, LANES), 0) < HEAD_DIM) == (iota((LANES, LANES), 1) < HEAD_DIM)


def block_diagonal(packed):
    return jnp.where(head_mask(), jnp.concatenate([packed, packed], axis=0), 0.0)


def pack_diagonal(full):
    left = iota((HEAD_DIM, LANES), 1) < HEAD_DIM
    return jnp.where(left, full[:HEAD_DIM], full[HEAD_DIM:])


def store_summary(place_ref, packed, rows, mine_ref, theirs_ref, extra=None):
    zero = on_core_zero(place_ref)
    half = len(packed) // 2
    first = iota((8, LANES), 0) == 0
    if extra is not None:
        at = slice(HEAD_DIM + 8, HEAD_DIM + 16)
        mine_ref[at, :] = jnp.zeros((8, mine_ref.shape[1]), f32)
        theirs_ref[at, :] = jnp.zeros((8, mine_ref.shape[1]), f32)
        mine_ref[at, :LANES] = jnp.where(zero, extra, 0.0)
        theirs_ref[at, :LANES] = jnp.where(zero, 0.0, extra)
    for p in range(half):
        at = slice(p * LANES, (p + 1) * LANES)
        low = jnp.concatenate([packed[p], jnp.where(first, rows[p], 0.0)], axis=0)
        high = jnp.concatenate([packed[p + half], jnp.where(first, rows[p + half], 0.0)], axis=0)
        mine_ref[: HEAD_DIM + 8, at] = jnp.where(zero, low, high)
        theirs_ref[: HEAD_DIM + 8, at] = jnp.where(zero, high, low)


def load_summary(place_ref, pair, pairs, mine_ref, theirs_ref):
    half = pairs // 2
    at = slice(pair % half * LANES, (pair % half + 1) * LANES)
    low, high = (mine_ref, theirs_ref) if pair < half else (theirs_ref, mine_ref)
    both = jnp.where(on_core_zero(place_ref), low[:, at], high[:, at])
    return both[:HEAD_DIM], both[HEAD_DIM : HEAD_DIM + 1]


def store_halves(place_ref, whole, mine_ref, theirs_ref, at):
    zero = on_core_zero(place_ref)
    rows = whole.shape[0] // 2
    low, high = whole[:rows], whole[rows:]
    mine_ref[:, at] = jnp.where(zero, low, high)
    theirs_ref[:, at] = jnp.where(zero, high, low).astype(bf16)


def send_row(send_ref):
    return jnp.concatenate([send_ref[p : p + 1, :] for p in range(send_ref.shape[0])], axis=1)


def start_kernel(
    place_ref,
    features_ref,
    wq_ref,
    wk_ref,
    wv_ref,
    send_ref,
    bases_ref,
    cot_ref,
    mine_ref,
    theirs_ref,
    out_ref,
    high_ref,
    low_ref,
    eq_ref,
    ek_ref,
    v_ref,
    *,
    arrive,
    leave,
):
    pairs = features_ref.shape[1] // LANES
    arrive(0)
    features = features_ref[...]
    arrive(1)
    eq_ref[...] = jnp.exp(mm(features, wq_ref[...]))
    leave(0)
    arrive(2)
    ek_ref[...] = jnp.exp(mm(features, wk_ref[...]))
    leave(1)
    arrive(3)
    v_ref[...] = mm(features, wv_ref[...])
    leave(2)
    packed, sums = [], []
    for p in range(pairs):
        at = slice(p * LANES, (p + 1) * LANES)
        key = ek_ref[:, at]
        packed.append(pack_diagonal(mm_wide(key, v_ref[:, at], TN)))
        sums.append(jnp.sum(key, axis=0, keepdims=True))
    store_summary(place_ref, packed, sums, mine_ref, theirs_ref)
    arrive(4)
    pick = one_hot_rows(send_row(send_ref), features.shape[0])
    out_ref[...] = mm(pick, features, TN).astype(bf16)
    arrive(5)
    arrive(6)
    cot = cot_ref[...].astype(bf16)
    for b in range(bases_ref.shape[0]):
        high, low = split(mm(cot, bases_ref[b], NT))
        for t in range(high_ref.shape[0]):
            high_ref[t, b * TILE : (b + 1) * TILE, :] = high[t * TILE : (t + 1) * TILE]
            low_ref[t, b * TILE : (b + 1) * TILE, :] = low[t * TILE : (t + 1) * TILE]


def attend_kernel(
    place_ref,
    eq_ref,
    cot_ref,
    sum_mine_ref,
    sum_theirs_ref,
    coef_ref,
    conv_ref,
    mine_ref,
    theirs_ref,
    qblock_ref,
    layer_ref,
    *,
    leave,
):
    pairs = eq_ref.shape[1] // LANES
    same_head = jnp.where(head_mask(), 1.0, 0.0).astype(bf16)
    packed, sums = [], []
    for p in range(pairs):
        at = slice(p * LANES, (p + 1) * LANES)
        kv, ks = load_summary(place_ref, p, pairs, sum_mine_ref, sum_theirs_ref)
        kv = block_diagonal(kv)
        query = eq_ref[:, at]
        cot = cot_ref[:, at]
        normalizer = mm_exact_right(query * ks, same_head)
        attended = mm_wide(query, kv) / normalizer
        layer_ref[:, at] = attended + conv_ref[:, at]
        num_grad = cot / normalizer
        den_grad = -mm_exact_right(cot * attended, same_head) / normalizer
        packed.append(pack_diagonal(mm_wide(query, num_grad, TN)))
        sums.append(jnp.sum(query * den_grad, axis=0, keepdims=True))
        query_side = mm_wide(num_grad, kv, NT) + den_grad * ks
        qblock_ref[:, at] = (query_side * query).astype(bf16)
    leave(0)
    store_summary(place_ref, packed, sums, mine_ref, theirs_ref, coef_ref[...])


def query_kernel(place_ref, qblock_ref, ek_ref, bases_theirs_ref, features_ref, mine_ref, theirs_ref):
    width = features_ref.shape[1]
    bases_width = bases_theirs_ref.shape[1]
    theirs_ref[:, :bases_width] = bases_theirs_ref[...]
    theirs_ref = theirs_ref.at[:, bases_width:]
    features = features_ref[...]
    store_halves(place_ref, mm(features, qblock_ref[...], TN), mine_ref, theirs_ref, slice(0, width))
    whole = mm_exact_left(features, ek_ref[...], TN)
    store_halves(place_ref, whole, mine_ref, theirs_ref, slice(width, 2 * width))


def key_kernel(
    place_ref, ek_ref, v_ref, sum_mine_ref, sum_theirs_ref, features_ref, kblock_ref, mine_ref, theirs_ref, *, arrive
):
    pairs = ek_ref.shape[1] // LANES
    for p in range(pairs):
        at = slice(p * LANES, (p + 1) * LANES)
        dkv, dks = load_summary(place_ref, p, pairs, sum_mine_ref, sum_theirs_ref)
        key_side = mm_wide(v_ref[:, at], block_diagonal(dkv), NT) + dks
        kblock_ref[:, at] = (key_side * ek_ref[:, at]).astype(bf16)
    arrive(0)
    store_halves(place_ref, mm(features_ref[...], kblock_ref[...], TN), mine_ref, theirs_ref, slice(None))


def returned_kernel(send_ref, table_ref, returned_ref, out_ref):
    rows = out_ref.shape[0]
    out_ref[...] = table_ref[:rows, :] + mm(one_hot_rows(send_row(send_ref), rows), returned_ref[...])


def input_grad_kernel(
    place_ref,
    qblock_ref,
    kblock_ref,
    ek_ref,
    sum_mine_ref,
    sum_theirs_ref,
    graph_ref,
    wq_ref,
    wk_ref,
    wv_ref,
    out_ref,
    token_ref,
):
    token_ref[...] = jnp.zeros((8, LANES), f32)
    pairs = ek_ref.shape[1] // LANES
    blocks = []
    for p in range(pairs):
        at = slice(p * LANES, (p + 1) * LANES)
        dkv, _ = load_summary(place_ref, p, pairs, sum_mine_ref, sum_theirs_ref)
        blocks.append(mm_wide(ek_ref[:, at], block_diagonal(dkv)).astype(bf16))
    total = mm(qblock_ref[...], wq_ref[...], NT) + mm(kblock_ref[...], wk_ref[...], NT)
    out_ref[...] = total + mm(jnp.concatenate(blocks, axis=1), wv_ref[...], NT) + graph_ref[...]


def tile_incidence(count_ref, dst_ref, tile):
    relations, _, slots = dst_ref.shape
    hits = []
    for r in range(relations):
        live = iota((TILE, slots), 1) < count_ref[r : r + 1, tile : tile + 1]
        target = iota((TILE, slots), 0) == dst_ref[r, tile : tile + 1, :]
        hits.append(jnp.where(target & live, 1.0, 0.0))
    ours = jnp.where(iota((relations * slots, LANES), 0) // slots == iota((relations * slots, LANES), 1), 1.0, 0.0)
    degree = mm(jnp.concatenate(hits, axis=1).astype(bf16), ours.astype(bf16))
    inverse = 1.0 / jnp.maximum(degree, 1.0)
    return [hit * inverse[:, r : r + 1] for r, hit in enumerate(hits)]


def tile_pick(src_ref, tile, table_rows):
    picks = [one_hot_rows(src_ref[r, tile : tile + 1, :], table_rows) for r in range(src_ref.shape[0])]
    return jnp.concatenate(picks, axis=1)


def backward_kernel(count_ref, coef_ref, src_ref, dst_ref, grad_ref, *refs, tile, last, leave):
    mixed_ref = refs[-1]
    table_ref = refs[0 if tile == 0 else 1]
    hits = tile_incidence(count_ref, dst_ref, tile)
    scaled = [
        jnp.concatenate([hit * coef_ref[r : r + 1, b : b + 1] for r, hit in enumerate(hits)], axis=1)
        for b in range(coef_ref.shape[1])
    ]
    high, low = split(jnp.concatenate(scaled, axis=0))
    both = mm(jnp.concatenate([high, low], axis=0), tile_pick(src_ref, tile, table_ref.shape[0]), NT)
    wide = both.shape[0] // 2
    high, low = split(both[:wide] + both[wide:])
    mixed_ref[:wide, :] = high
    mixed_ref[wide:, :] = low
    leave(0)
    table = mm(high, grad_ref[tile], TN)
    table = table if tile == 0 else table + refs[0][...]
    table_ref[...] = table
    if last:
        sent_ref = refs[-2]
        sent_ref[...] = table[table.shape[0] - sent_ref.shape[0] :, :].astype(bf16)


def forward_kernel(count_ref, place_ref, src_ref, dst_ref, *refs, arrive):
    relations, tiles, slots = src_ref.shape
    own_ref, halo_ref, high_ref, low_ref, bases_ref = refs[:5]
    mixed_refs, refs = refs[5 : 5 + tiles], refs[5 + tiles :]
    cot_ref, conv_ref, coef_grad_ref, mine_ref, theirs_ref, basis_ref, table_ref = refs
    basis_count = bases_ref.shape[0]
    wide = basis_count * TILE
    rows, width = own_ref.shape
    sums = [jnp.zeros((1, relations * slots), f32) for _ in range(basis_count)]
    for t in range(tiles):
        hit = jnp.concatenate(tile_incidence(count_ref, dst_ref, t), axis=1)
        pick = tile_pick(src_ref, t, table_ref.shape[0])
        if t == 0:
            for i in range(4):
                arrive(i)
            table_ref[:rows, :] = own_ref[...]
            table_ref[rows:, :] = halo_ref[...]
        dots = mm(jnp.concatenate([high_ref[t], low_ref[t]], axis=0), table_ref[...], NT)
        edge = mm((dots[:wide] + dots[wide:]).astype(bf16), pick)
        for b in range(basis_count):
            sums[b] += jnp.sum(edge[b * TILE : (b + 1) * TILE] * hit, axis=0, keepdims=True)
        if t == 0:
            arrive(4)
        arrive(5 + t)
        both = mm(mixed_refs[t][...], table_ref[...])
        both = (both[:wide] + both[wide:]).astype(bf16)
        at = slice(t * TILE, (t + 1) * TILE)
        conv = None
        for b in range(basis_count):
            basis_in = both[b * TILE : (b + 1) * TILE]
            basis_ref[b, at, :] = basis_in
            part = mm(basis_in, bases_ref[b])
            conv = part if conv is None else conv + part
        conv_ref[at, :] = conv
    row, lane = iota((8, LANES), 0), iota((8, LANES), 1)
    total = jnp.zeros((8, LANES), f32)
    for b in range(basis_count):
        for r in range(relations):
            part = jnp.sum(sums[b][:, r * slots : (r + 1) * slots], axis=1, keepdims=True)
            total = jnp.where((row == r) & (lane == b), part, total)
    coef_grad_ref[...] = total
    arrive(5 + tiles)
    cot = cot_ref[...].astype(bf16)
    for b in range(basis_count):
        whole = mm(basis_ref[b], cot, TN)
        store_halves(place_ref, whole, mine_ref, theirs_ref, slice(b * width, (b + 1) * width))


def copy_kernel(a_ref, out_ref):
    out_ref[...] = a_ref[...]


def add_kernel(a_ref, b_ref, out_ref):
    out_ref[...] = a_ref[...] + b_ref[...]


def choose(place_ref, first_bit, blocks, index):
    bit = first_bit
    while len(blocks) > 1:
        zero = bit_is_zero(place_ref, bit)
        pairs = [(blocks[i], blocks[i + 1]) for i in range(0, len(blocks), 2)]
        if index % 2:
            blocks = [jnp.where(zero, high, low) for low, high in pairs]
        else:
            blocks = [jnp.where(zero, low, high) for low, high in pairs]
        index //= 2
        bit += 1
    return blocks[0]


def scatter_kernel(place_ref, *refs, first_bit, beside, others):
    pieces, others = refs[:beside], refs[beside : beside + others]
    keep_ref, *send_refs = refs[beside + len(others) :]
    rows = keep_ref.shape[0]
    count = len(send_refs) + 1
    at = 0
    for piece in pieces:
        lanes = slice(at, at + piece.shape[1])
        blocks = []
        for i in range(count):
            rows_at = slice(i * rows, (i + 1) * rows)
            block = piece[rows_at, :].astype(f32)
            for other in others:
                block += other[rows_at, lanes].astype(f32)
            blocks.append(block)
        keep_ref[:, lanes] = choose(place_ref, first_bit, blocks, 0)
        for k in range(1, count):
            send_refs[k - 1][:, lanes] = choose(place_ref, first_bit, blocks, k).astype(send_refs[k - 1].dtype)
        at += piece.shape[1]


def total_kernel(*refs):
    out_ref = refs[-1]
    total = refs[0][...].astype(f32)
    for ref in refs[1:-1]:
        total += ref[...].astype(f32)
    out_ref[...] = total.astype(out_ref.dtype)


def join_kernel(place_ref, *refs, first_bit):
    out_ref = refs[-1]
    blocks = [ref[...] for ref in refs[:-1]]
    rows = blocks[0].shape[0]
    for i in range(len(blocks)):
        out_ref[i * rows : (i + 1) * rows, :] = choose(place_ref, first_bit, blocks, i).astype(out_ref.dtype)


def finish_kernel(
    place_ref, sum_mine_ref, sum_theirs_ref, mine_ref, theirs_ref, *refs, scale, value_at, outs, after
):
    refs = refs[after:]
    refs[outs][...] = jnp.zeros((8, LANES), f32)
    holds, sems = refs[outs + 1 : -1], refs[-1]
    targets = []
    for out_ref in refs[:outs]:
        targets += [out_ref] if len(out_ref.shape) == 2 else [out_ref.at[b] for b in range(out_ref.shape[0])]
    zero = on_core_zero(place_ref)
    rows = mine_ref.shape[0]
    width = holds[0].shape[1]
    moves = []
    for i, hold in enumerate(holds):
        for p in range(width // LANES):
            at = slice(p * LANES, (p + 1) * LANES)
            source = slice(i * width + p * LANES, i * width + (p + 1) * LANES)
            if i == value_at:
                dkv, _ = load_summary(place_ref, p, width // LANES, sum_mine_ref, sum_theirs_ref)
                dkv = block_diagonal(dkv)
                a = mm_exact_left(mine_ref[:, source], dkv) * scale
                b = mm_exact_left(theirs_ref[:, source], dkv) * scale
            else:
                a = mine_ref[:, source].astype(f32) * scale
                b = theirs_ref[:, source].astype(f32) * scale
            hold[:rows, at] = jnp.where(zero, a, b)
            hold[rows:, at] = jnp.where(zero, b, a)
        moves.append(pltpu.make_async_copy(hold, targets[i], sems.at[i]))
        moves[-1].start()
    for move in moves:
        move.wait()


def swap_cores(x):
    return lax.ppermute(x, "outer", [(0, 1), (1, 0)])


def swap_nodes(x, bit):
    nodes = lax.axis_size("nodes")
    return lax.ppermute(x, "nodes", [(i, i ^ (1 << bit)) for i in range(nodes)])


def run_all(plan, step, x):
    return [y for y in [run(x) for run in plan.get(step, [])] if y is not None]


def sum_summary(mine, theirs, bits, beside):
    out = [shape(*mine.shape)]
    received = swap_cores(theirs)
    (mine,) = call(add_kernel, out, [mine, received], beside("core", mine))
    for bit in bits:
        received = swap_nodes(mine, bit)
        (mine,) = call(add_kernel, out, [mine, received], beside(bit, mine))
    return mine, swap_cores(mine), beside("back", mine)


def exchange(sends, first_bit):
    nodes = lax.axis_size("nodes")
    return [
        lax.ppermute(x, "nodes", [(i, i ^ (k << first_bit)) for i in range(nodes)])
        for k, x in enumerate(sends, start=1)
    ]


def per_device(
    features, w_query, w_key, w_value, bases, rel_coef, send_rows, tile_src, tile_dst, tile_count, cotangent
):
    rows, width = features.shape
    nodes = lax.axis_size("nodes")
    scale = 1.0 / math.sqrt(rows * nodes * lax.axis_size("outer"))
    basis_count = bases.shape[0]
    slots = send_rows.shape[2]
    halo_rows = nodes * slots
    table_rows = rows + halo_rows
    core, node = lax.axis_index("outer"), lax.axis_index("nodes")
    place = jnp.stack([core] + [(node >> bit) & 1 for bit in range(7)]).astype(jnp.int32)
    place = jnp.broadcast_to(place[:, None], (8, LANES))
    send, src, dst, count = send_rows[0], tile_src[0], tile_dst[0], tile_count[0]
    relations, tiles, cap = src.shape
    bits = list(range(nodes.bit_length() - 1))
    y, z1, z2 = bits[-3:]

    square, square_half = shape(rows, width), shape(rows, width, dtype=bf16)
    summary = shape(HEAD_DIM + 8, width // 2)
    wide_summary = shape(HEAD_DIM + 16, width // 2)

    def halves(n):
        return shape(width // 2, n * width), shape(width // 2, n * width, dtype=bf16)

    grads = shape(tiles, basis_count * TILE, width, dtype=bf16)
    kv_mine, kv_theirs, outgoing, grad_high, grad_low, exp_query, exp_key, values = call(
        start_kernel,
        [summary, summary, shape(halo_rows, width, dtype=bf16), grads, grads],
        [place],
        (),
        16,
        far=[features, w_query, w_key, w_value, send, bases, cotangent],
        us=5.5,
        lazy=True,
        far_outs=[square, square, square],
    )
    halo = lax.all_to_all(
        outgoing.reshape(nodes, slots, width), "nodes", split_axis=0, concat_axis=0, tiled=True
    ).reshape(halo_rows, width)

    kept = {}

    def run_backward(t, x):
        last = t == tiles - 1
        sent = [shape(halo_rows, width, dtype=bf16)] if last else []
        kept["table"], *sent, kept["mixed", t] = call(
            functools.partial(backward_kernel, tile=t, last=last),
            [shape(table_rows, width), *sent],
            [count, rel_coef, src, dst, grad_high] + ([kept["table"]] if t > 0 else []),
            [x],
            table_rows // 64,
            us=2.1,
            far_outs=[shape(2 * basis_count * TILE, table_rows, dtype=bf16)],
        )
        if last:
            kept["returned"] = lax.all_to_all(
                sent[0].reshape(nodes, slots, width), "nodes", split_axis=0, concat_axis=0, tiled=True
            ).reshape(halo_rows, width)
        return kept["table"]

    def run_forward(x):
        kept["conv"], kept["coef"], *kept["bases"] = call(
            forward_kernel,
            [square, shape(8, LANES), *halves(basis_count)],
            [count, place, src, dst],
            [x],
            8 + table_rows // 64,
            far=[features, halo, grad_high, grad_low, bases, *[kept["mixed", t] for t in range(tiles)], cotangent],
            us=9,
            lazy=True,
            scratch=[shape(basis_count, rows, width, dtype=bf16), shape(table_rows, width, dtype=bf16)],
        )
        return None

    backward = [functools.partial(run_backward, t) for t in range(tiles)]
    first = {bits[0]: backward[:1], y: backward[1:2], z1: backward[2:3], z2: backward[3:], "back": [run_forward]}
    kv_mine, kv_theirs, after = sum_summary(
        kv_mine, kv_theirs, bits, functools.partial(run_all, first)
    )
    dkv_mine, dkv_theirs, qblock, layer_out = call(
        attend_kernel,
        [wide_summary, wide_summary, square_half],
        [place, exp_query, cotangent, kv_mine, kv_theirs, kept["coef"], kept["conv"]],
        after,
        us=2.7,
        far_outs=[square],
    )

    plane, planes = nodes // 4, 4
    plane_rows = width // 2 // plane
    place_rows = plane_rows // planes
    early_count = basis_count + 2
    early_width = early_count * width

    def scatter(operands, first_bit, count, n_rows, beside=1, after=()):
        columns = sum(x.shape[1] for x in operands[:beside])
        own, *out = call(
            functools.partial(
                scatter_kernel, first_bit=first_bit, beside=beside, others=len(operands) - beside
            ),
            [shape(n_rows, columns)] + [shape(n_rows, columns, dtype=bf16 if n_rows >= 16 else f32)] * (count - 1),
            [place, *operands],
            after,
            12,
        )
        return [own, *exchange(out, first_bit)]

    def join(blocks, first_bit, after=()):
        own = blocks[0]
        rows = len(blocks) * own.shape[0]
        outs = [shape(rows, own.shape[1], dtype=bf16 if rows >= 16 else f32)]
        return call(functools.partial(join_kernel, first_bit=first_bit), outs, [place, *blocks], after)[0]

    def total(blocks, after=()):
        out = shape(*blocks[0].shape, dtype=bf16 if blocks[0].shape[0] >= 16 else f32)
        return call(total_kernel, [out], blocks, after)[0]

    def finish(own, bodies, value_at, after=()):
        count = sum(max(n, 1) for n in bodies)
        return pl.pallas_call(
            functools.partial(finish_kernel, scale=scale, value_at=value_at, outs=len(bodies), after=len(after)),
            out_shape=[shape(n, width, width) if n else shape(width, width) for n in bodies] + [shape(8, LANES)],
            in_specs=[VMEM] * (5 + len(after)),
            out_specs=[HBM] * len(bodies) + [VMEM],
            scratch_shapes=[pltpu.VMEM((width, width), f32)] * count + [pltpu.SemaphoreType.DMA((count,))],
            compiler_params=pltpu.CompilerParams(vmem_limit_bytes=12 * 1024 * 1024),
            cost_estimate=pl.CostEstimate(flops=int(count * 0.8e9), bytes_accessed=0, transcendentals=0),
        )(place, dkv_mine, dkv_theirs, own, swap_cores(own), *after)

    def run_returned(x):
        (kept["graph"],) = call(
            returned_kernel, [square], [send, kept["table"], kept["returned"]], [x], us=0.5
        )
        return kept["graph"]

    def run_query(x):
        kept["early"] = call(
            query_kernel,
            [halves(2)[0], halves(early_count)[1]],
            [place, qblock, exp_key, kept["bases"][1]],
            [x],
            12,
            far=[features],
            us=1.8,
        )
        return kept["early"][1]

    def run_early_plane(x):
        operands = [kept["bases"][0], kept["early"][0], swap_cores(kept["early theirs"])]
        kept["blocks"] = scatter(operands, 0, plane, plane_rows, 2, [x])
        return kept["blocks"][0]

    def run_early_line(x):
        kept["blocks"] = scatter(kept["blocks"], z1, planes, place_rows, 1, [x])
        return kept["blocks"][0]

    def run_early_theirs(x):
        (kept["early theirs"],) = call(copy_kernel, [halves(early_count)[1]], [kept["early"][1]], [x])
        return kept["early theirs"]

    second = {"core": [run_returned], bits[0]: [run_query], y: [run_early_theirs], z1: [run_early_plane]}
    second["back"] = [run_early_line]
    dkv_mine, dkv_theirs, after = sum_summary(dkv_mine, dkv_theirs, bits, functools.partial(run_all, second))
    kblock, key_mine, key_theirs = call(
        key_kernel,
        [square_half, *halves(1)],
        [place, exp_key, values, dkv_mine, dkv_theirs],
        after,
        far=[features],
        us=1.3,
        lazy=True,
    )
    def spread(x, first_bit, count):
        return [x, *exchange([x] * (count - 1), first_bit)]

    key = scatter([key_mine, swap_cores(key_theirs)], 0, plane, plane_rows)
    early = spread(total(kept["blocks"], [key[0]]), z1, planes)
    key = spread(total(key, [early[0]]), z1, planes)
    early = join(early, z1, [key[0]])
    key = spread(total(key), 0, plane)
    early = spread(early, 0, plane)
    key = join(key, 0, [early[0]])
    grad_x, token = call(
        input_grad_kernel,
        [square, shape(8, LANES)],
        [place, qblock, kblock, exp_key, dkv_mine, dkv_theirs, kept["graph"]],
        [key],
        16,
        far=[w_query, w_key, w_value],
        us=3.5,
    )
    key_grad, done = finish(key, [0], -1)
    early = join(early, 0, [token, done])
    bases_grad, query_grad, value_grad, _ = finish(early, [basis_count, 0, 0], basis_count + 1)
    coef_sum = jnp.where(core == 0, dkv_mine, dkv_theirs)[HEAD_DIM + 8 :, :]
    coef_grad = coef_sum[:relations, :basis_count] * scale
    return layer_out, grad_x, query_grad, key_grad, value_grad, bases_grad, coef_grad


def solution(mesh):
    both = ("outer", "nodes")
    in_specs = (
        P(both, None),
        P(),
        P(),
        P(),
        P(),
        P(),
        P(both, None, None),
        P(both, None, None, None),
        P(both, None, None, None),
        P(both, None, None),
        P(both, None),
    )
    out_specs = (P(both, None), P(both, None), P(), P(), P(), P(), P())
    return jax.shard_map(per_device, mesh=mesh, in_specs=in_specs, out_specs=out_specs, check_vma=False)
```
